128 devices in a mesh: lat: 16 (over x_hi, z, core), lon: 8 (over y, x_lo).
Axes of the slice: x: 4 (x_hi: 2, x_lo: 2; x = x_hi * 2 + x_lo), y: 4, z: 4, core: 2. Of those that a mesh axis runs over, the one named last changes fastest.
Arguments:
- pedersen: float32 [16, 2048, 4096], P(None, 'lat', 'lon'), may hold values from 0.2 to 2
- hall_conductivity: float32 [16, 2048, 4096], P(None, 'lat', 'lon'), may hold values from 0.1 to 1.5
- east_wind: float32 [16, 2048, 4096], P(None, 'lat', 'lon'), may hold values from -6 to 6
- north_wind: float32 [16, 2048, 4096], P(None, 'lat', 'lon'), may hold values from -6 to 6
- ion_density: float32 [3, 2048, 4096], P(None, 'lat', 'lon'), may hold values from 0.5 to 2
Outputs:
- potential: float32 [2048, 4096], P('lat', 'lon')
- ion_update: float32 [3, 2048, 4096], P(None, 'lat', 'lon')
The draws below stay inside these ranges and needn't reach their ends.
All inputs are finite; a program needn't handle non-finite values. Where the reference program divides by a largest or mean magnitude, that divisor is 1e-20 or more.
Results may differ from the reference program's by a relative error of at most 0.00002.
Values sent between devices are 32-bit elements; how exact they have to be, the bound alone decides.
No kernel may reach another device: no remote copies, remote signals or barrier semaphores. Data moves between devices by JAX's collectives and lax.ppermute only.
A program may use at most 192 MiB of HBM per device.

```python
import math
import jax
import jax.numpy as jnp
from jax import lax

LEV = 16
SWEEPS = 16
NLAT = 2048
NLON = 4096


def steps_of(own_key, extent, pieces, least, top_value):
    level, own = 1.0, jax.random.fold_in(own_key, 6)
    for axis_at, shards_of in pieces:
        heights = jnp.exp(jax.random.uniform(jax.random.fold_in(own, axis_at), (shards_of,), jnp.float32, least / len(pieces), top_value / len(pieces)))
        level = level * jnp.repeat(heights, extent[axis_at] // shards_of).reshape([-1 if axis == axis_at else 1 for axis in range(len(extent))])
    return level


def bell_draw(rng, extent, scale, bound, split=(), kind=jnp.bfloat16):
    entries = scale * jax.random.normal(rng, extent, jnp.float32)
    if split:
        entries = entries * steps_of(rng, extent, split, -0.22, 0.18)
    return jnp.clip(entries, -bound, bound).astype(kind)


def setup_inputs(seed: int = 0) -> dict:
    key_list = jax.random.split(jax.random.key(seed), 6)
    return {
        "pedersen": jnp.clip(jnp.exp(math.log(2.0) - 2.3025851 * jax.random.uniform(key_list[0], (LEV, NLAT, NLON), jnp.float32) ** steps_of(key_list[0], (LEV, NLAT, NLON), ((1, 16), (2, 8)), -0.2, 0.2)), 0.2, 2.0),
        "hall_conductivity": jnp.clip(jnp.exp(math.log(1.5) - 2.7080502 * jax.random.uniform(key_list[1], (LEV, NLAT, NLON), jnp.float32) ** steps_of(key_list[1], (LEV, NLAT, NLON), ((1, 16), (2, 8)), -0.2, 0.2)), 0.1, 1.5),
        "east_wind": bell_draw(key_list[2], (LEV, NLAT, NLON), 1.0, 6.0, ((1, 16), (2, 8)), jnp.float32),
        "north_wind": bell_draw(key_list[3], (LEV, NLAT, NLON), 1.0, 6.0, ((1, 16), (2, 8)), jnp.float32),
        "ion_density": jnp.clip(jnp.exp(math.log(2.0) - 1.3862944 * jax.random.uniform(key_list[4], (3, NLAT, NLON), jnp.float32) ** steps_of(key_list[4], (3, NLAT, NLON), ((1, 16), (2, 8)), -0.2, 0.2)), 0.5, 2.0),
    }


DAMPING = 0.0001
LOW_BOUND = 0.05
HIGH_BOUND = 2.0
COURANT = 0.8
MOBILITY = (1.0, 0.6, 0.3)
NEIGHBOURS = ((-1, 0, 1.0), (1, 0, 1.0), (0, -1, 1.0), (0, 1, 1.0), (-1, -1, 0.5), (-1, 1, 0.5), (1, -1, 0.5), (1, 1, 0.5))


def thickness():
    levels = jnp.arange(LEV, dtype=jnp.float32)
    return (0.5 + levels / LEV) / LEV


def chebyshev_factors():
    theta = 0.5 * (HIGH_BOUND + LOW_BOUND)
    delta = 0.5 * (HIGH_BOUND - LOW_BOUND)
    sigma_one = theta / delta
    rho_prev = 1.0 / sigma_one
    first_list = []
    second_list = []
    for sweep in range(SWEEPS):
        rho_next = 1.0 / (2.0 * sigma_one - rho_prev)
        first_list.append(rho_next * rho_prev)
        second_list.append(2.0 * rho_next / delta)
        rho_prev = rho_next
    return theta, first_list, second_list


def extend(field, width):
    padded = jnp.pad(field, ((width, width), (0, 0)))
    return jnp.concatenate([padded[:, -width:], padded, padded[:, :width]], axis=1)


def window(array, shift_lat, shift_lon):
    height = array.shape[0] - 2
    breadth = array.shape[1] - 2
    return array[1 + shift_lat:1 + shift_lat + height, 1 + shift_lon:1 + shift_lon + breadth]


def stencil(sigma_ext):
    center = window(sigma_ext, 0, 0)
    weights = []
    diagonal = jnp.zeros_like(center) + DAMPING
    for shift_lat, shift_lon, factor in NEIGHBOURS:
        weight = factor * 0.5 * (center + window(sigma_ext, shift_lat, shift_lon))
        weights.append(weight)
    for weight in weights:
        diagonal = diagonal + weight
    return weights, diagonal


def apply_operator(field_ext, weights, diagonal):
    result = diagonal * window(field_ext, 0, 0)
    for index_pair, (shift_lat, shift_lon, factor) in enumerate(NEIGHBOURS):
        result = result - weights[index_pair] * window(field_ext, shift_lat, shift_lon)
    return result


def divergence(east_ext, north_ext):
    return 0.5 * (window(east_ext, 0, 1) - window(east_ext, 0, -1)) + 0.5 * (window(north_ext, 1, 0) - window(north_ext, -1, 0))


def advect(density_ext, cross_east, cross_north):
    density = window(density_ext, 0, 0)
    result = density - jnp.maximum(cross_east, 0.0) * (density - window(density_ext, 0, -1))
    result = result - jnp.minimum(cross_east, 0.0) * (window(density_ext, 0, 1) - density)
    result = result - jnp.maximum(cross_north, 0.0) * (density - window(density_ext, -1, 0))
    result = result - jnp.minimum(cross_north, 0.0) * (window(density_ext, 1, 0) - density)
    return result


def reference(pedersen, hall_conductivity, east_wind, north_wind, ion_density):
    layer = thickness()

    def accumulate(level, totals):
        sigma_p = pedersen[level]
        sigma_h = hall_conductivity[level]
        wind_e = east_wind[level]
        wind_n = north_wind[level]
        return (totals[0] + layer[level] * sigma_p,
                totals[1] + layer[level] * (sigma_p * wind_e + sigma_h * wind_n),
                totals[2] + layer[level] * (sigma_p * wind_n - sigma_h * wind_e))

    zeros = jnp.zeros(pedersen.shape[1:], jnp.float32)
    sigma, current_east, current_north = lax.fori_loop(0, LEV, accumulate, (zeros, zeros, zeros))
    sigma = sigma + sigma[::-1]
    current_east = current_east + current_east[::-1]
    current_north = current_north + current_north[::-1]
    weights, diagonal = stencil(extend(sigma, 1))
    source = divergence(extend(current_east, 1), extend(current_north, 1))
    theta, first_list, second_list = chebyshev_factors()
    solution = jnp.zeros_like(source)
    update = source / diagonal / theta
    for sweep in range(SWEEPS):
        solution = solution + update
        image = apply_operator(extend(solution, 1), weights, diagonal)
        scaled = (source - image) / diagonal
        update = first_list[sweep] * update + second_list[sweep] * scaled
    potential = solution
    potential_ext = extend(potential, 1)
    drift_east = -0.5 * (window(potential_ext, 1, 0) - window(potential_ext, -1, 0))
    drift_north = 0.5 * (window(potential_ext, 0, 1) - window(potential_ext, 0, -1))
    fastest = jnp.max(jnp.abs(drift_east) + jnp.abs(drift_north))
    time_step = COURANT / (fastest + 1e-6)
    results = []
    for species in range(3):
        cross_east = MOBILITY[species] * time_step * drift_east
        cross_north = MOBILITY[species] * time_step * drift_north
        results.append(advect(extend(ion_density[species], 1), cross_east, cross_north))
    return potential, jnp.stack(results)
```

```python
import functools

import jax
import jax.numpy as jnp
from jax import lax
from jax.experimental import pallas as pl
from jax.experimental.pallas import tpu as pltpu
from jax.sharding import PartitionSpec as P

LEV = 16
SWEEPS = 16
DAMPING = 0.0001
LOW_BOUND = 0.05
HIGH_BOUND = 2.0
COURANT = 0.8
MOBILITY = (1.0, 0.6, 0.3)

LANES = 128
ROWS = 128
COLS = 512
TILES = COLS // LANES
EDGE = 24
SIDE = 32
MID = ROWS - 2 * EDGE
EXT = ROWS + 2 * EDGE
BAND = 2 * EDGE + 8
STRIP = ROWS + 8
CHUNK = 16
VMEM_BYTES = 48 * 1024 * 1024


def chebyshev_factors():
    theta = 0.5 * (HIGH_BOUND + LOW_BOUND)
    delta = 0.5 * (HIGH_BOUND - LOW_BOUND)
    sigma_one = theta / delta
    rho_prev = 1.0 / sigma_one
    first_list = []
    second_list = []
    for sweep in range(SWEEPS):
        rho_next = 1.0 / (2.0 * sigma_one - rho_prev)
        first_list.append(rho_next * rho_prev)
        second_list.append(2.0 * rho_next / delta)
        rho_prev = rho_next
    return (theta, first_list, second_list)


def lane_index(rows):
    return lax.broadcasted_iota(jnp.int32, (rows, LANES), 1)


def row_index(rows, cols=LANES):
    return lax.broadcasted_iota(jnp.int32, (rows, cols), 0)


def reversed_rows(tile):
    row = row_index(8, tile.shape[1])
    tile = pltpu.roll(tile, 4, 0)
    tile = jnp.where((row & 2) == 0, pltpu.roll(tile, 6, 0), pltpu.roll(tile, 2, 0))
    return jnp.where((row & 1) == 0, pltpu.roll(tile, 7, 0), pltpu.roll(tile, 1, 0))


def shifted(tiles, to_right):
    count = len(tiles)
    lane = lane_index(tiles[0].shape[0])
    if to_right:
        turned = [pltpu.roll(tile, 1, 1) for tile in tiles]
        return [jnp.where(lane == 0, turned[t - 1], turned[t]) for t in range(count)]
    turned = [pltpu.roll(tile, LANES - 1, 1) for tile in tiles]
    return [jnp.where(lane == LANES - 1, turned[(t + 1) % count], turned[t]) for t in range(count)]


def local_source(east, north, source, start, rows):
    tiles = [east[start : start + rows, t * LANES : (t + 1) * LANES] for t in range(TILES)]
    lane = lane_index(rows)
    row = row_index(rows)
    left = [pltpu.roll(tile, 1, 1) for tile in tiles]
    right = [pltpu.roll(tile, LANES - 1, 1) for tile in tiles]
    zero = jnp.zeros((rows, LANES), jnp.float32)
    for t in range(TILES):
        span = slice(t * LANES, (t + 1) * LANES)
        before = jnp.where(lane == 0, left[t - 1] if t else zero, left[t])
        after = jnp.where(lane == LANES - 1, right[t + 1] if t < TILES - 1 else zero, right[t])
        here = north[start : start + rows, span]
        up = pltpu.roll(here, 1, 0)
        down = pltpu.roll(here, rows - 1, 0)
        above = north[start - 8 : start, span][7:8] if start else zero[:1]
        below = north[start + rows : start + rows + 8, span][:1] if start + rows < ROWS else zero[:1]
        up = jnp.where(row == 0, above, up)
        down = jnp.where(row == rows - 1, below, down)
        source[start : start + rows, span] = 0.5 * (after - before) + 0.5 * (down - up)


def write_pieces(sigma, east, north, source, strips, bands, middle):
    for start in range(0, ROWS, 8):
        local_source(east, north, source, start, 8)
    lane = lane_index(ROWS)
    last = COLS - LANES
    strips[0, :ROWS] = jnp.where(
        lane < SIDE,
        sigma[:, :LANES],
        jnp.where(
            lane < 2 * SIDE,
            pltpu.roll(source[:, :LANES], SIDE, 1),
            jnp.where(lane == LANES - 1, pltpu.roll(east[:, :LANES], LANES - 1, 1), 0.0),
        ),
    )
    strips[1, :ROWS] = jnp.where(
        lane >= LANES - SIDE,
        sigma[:, last:],
        jnp.where(
            lane >= LANES - 2 * SIDE,
            pltpu.roll(source[:, last:], LANES - SIDE, 1),
            jnp.where(lane == 0, pltpu.roll(east[:, last:], 1, 1), 0.0),
        ),
    )
    row = row_index(8)
    for side, at in ((0, 0), (1, last)):
        span = slice(at, at + LANES)
        strips[side, ROWS:] = jnp.where(
            row == 0, north[0:8, span][:1], jnp.where(row == 1, north[ROWS - 8 :, span][7:8], 0.0)
        )
    wide = row_index(8, COLS)
    for side, at in ((0, 0), (1, ROWS - EDGE)):
        bands[side, :EDGE] = sigma[at : at + EDGE]
        bands[side, EDGE : 2 * EDGE] = source[at : at + EDGE]
        line = north[0:8][:1] if side == 0 else north[ROWS - 8 :][7:8]
        bands[side, 2 * EDGE :] = jnp.where(wide == 0, line, 0.0)
    middle[0] = sigma[EDGE : ROWS - EDGE]
    middle[1] = source[EDGE : ROWS - EDGE]


def column_kernel(
    pedersen, hall, east_wind, north_wind,
    own_strips, own_bands, own_middle, far_strips, far_bands, far_middle,
    sigma, east, north, sigma_far, east_far, north_far, source,
):
    step = pl.program_id(0)
    steps = ROWS // CHUNK
    for half in range(CHUNK // 8):
        span = slice(half * 8, half * 8 + 8)
        totals = [jnp.zeros((8, COLS), jnp.float32) for _ in range(3)]
        for level in range(LEV):
            layer = (0.5 + level / LEV) / LEV
            along = layer * pedersen[level, span, :]
            across = layer * hall[level, span, :]
            wind_e = east_wind[level, span, :]
            wind_n = north_wind[level, span, :]
            totals[0] = totals[0] + along
            totals[1] = totals[1] + (along * wind_e + across * wind_n)
            totals[2] = totals[2] + (along * wind_n - across * wind_e)
        near = pl.ds(pl.multiple_of(step * CHUNK + half * 8, 8), 8)
        away = pl.ds(pl.multiple_of((steps - 1 - step) * CHUNK + CHUNK - 8 - half * 8, 8), 8)
        for total, here, there in zip(totals, (sigma, east, north), (sigma_far, east_far, north_far)):
            here[near, :] = total
            there[away, :] = reversed_rows(total)

    @pl.when(step == steps - 1)
    def _():
        write_pieces(sigma_far, east_far, north_far, source, far_strips, far_bands, far_middle)
        write_pieces(sigma, east, north, source, own_strips, own_bands, own_middle)


def column_sums(pedersen, hall, east_wind, north_wind):
    block = pl.BlockSpec((LEV, CHUNK, COLS), lambda i: (0, i, 0))
    shapes = [(2, STRIP, LANES), (2, BAND, COLS), (2, MID, COLS)] * 2
    field = pltpu.VMEM((ROWS, COLS), jnp.float32)
    return pl.pallas_call(
        column_kernel,
        grid=(ROWS // CHUNK,),
        in_specs=[block] * 4,
        out_specs=[pl.BlockSpec(shape, lambda i: (0, 0, 0)) for shape in shapes],
        out_shape=[jax.ShapeDtypeStruct(shape, jnp.float32) for shape in shapes],
        scratch_shapes=[field] * 7,
        compiler_params=pltpu.CompilerParams(vmem_limit_bytes=VMEM_BYTES),
        name="column_sums",
    )(pedersen, hall, east_wind, north_wind)


def strip_kernel(own, far, ions_first, ions_last, to_left, to_right):
    lane = lane_index(ROWS)
    left = own[0, :ROWS] + far[0, :ROWS]
    right = own[1, :ROWS] + far[1, :ROWS]
    for s in range(3):
        left = jnp.where(lane == 2 * SIDE + s, pltpu.roll(ions_first[s], 2 * SIDE + s, 1), left)
        right = jnp.where(lane == SIDE + s, pltpu.roll(ions_last[s], SIDE + s + 1, 1), right)
    to_left[:ROWS] = left
    to_right[:ROWS] = right
    to_left[ROWS:] = own[0, ROWS:] + far[0, ROWS:]
    to_right[ROWS:] = own[1, ROWS:] + far[1, ROWS:]


def strips_to_send(own, far, ions):
    whole = pl.BlockSpec((2, STRIP, LANES), lambda i: (0, 0, 0))
    shape = jax.ShapeDtypeStruct((STRIP, LANES), jnp.float32)
    return pl.pallas_call(
        strip_kernel,
        grid=(1,),
        in_specs=[
            whole,
            whole,
            pl.BlockSpec((3, ROWS, LANES), lambda i: (0, 0, 0)),
            pl.BlockSpec((3, ROWS, LANES), lambda i: (0, 0, TILES - 1)),
        ],
        out_specs=[pl.BlockSpec((STRIP, LANES), lambda i: (0, 0))] * 2,
        out_shape=[shape, shape],
        name="lon_strips",
    )(own, far, ions, ions)


def halo_sigma(from_right, from_left):
    lane = lane_index(from_right.shape[0])
    return jnp.where(lane < SIDE, from_right, jnp.where(lane >= LANES - SIDE, from_left, 0.0))


def halo_source(from_right, from_left, own_left, own_right):
    lane = lane_index(from_right.shape[0])
    tile = jnp.where(
        lane < SIDE,
        pltpu.roll(from_right, LANES - SIDE, 1),
        jnp.where(lane >= LANES - SIDE, pltpu.roll(from_left, SIDE, 1), 0.0),
    )
    tile = tile - jnp.where(lane == 0, 0.5 * own_right, 0.0)
    return tile + jnp.where(lane == LANES - 1, 0.5 * own_left, 0.0)


def first_fix(from_left):
    return jnp.where(lane_index(from_left.shape[0]) == 0, -0.5 * from_left, 0.0)


def last_fix(from_right):
    return jnp.where(lane_index(from_right.shape[0]) == LANES - 1, 0.5 * from_right, 0.0)


def band_kernel(own, far, own_left, own_right, from_right, from_left, ions_top, ions_bottom, top, bottom):
    for side, out, start in ((0, top, 0), (1, bottom, ROWS - EDGE)):
        rows = slice(start, start + EDGE)
        out[:, :COLS] = own[side] + far[side]
        out[:EDGE, COLS:] = halo_sigma(from_right[rows], from_left[rows])
        out[EDGE : 2 * EDGE, COLS:] = halo_source(
            from_right[rows], from_left[rows], own_left[rows], own_right[rows]
        )
        part = slice(EDGE, 2 * EDGE)
        out[part, :LANES] += first_fix(from_left[rows])
        out[part, COLS - LANES : COLS] += last_fix(from_right[rows])
        extra = halo_sigma(from_right[ROWS:], from_left[ROWS:])
        out[2 * EDGE :, COLS:] = jnp.where(row_index(8) == 0, extra[side : side + 1], 0.0)
        ions = ions_top if side == 0 else ions_bottom
        wide = row_index(8, COLS)
        lines = out[2 * EDGE :, :COLS]
        for s in range(3):
            line = ions[s, 0:1] if side == 0 else ions[s, 7:8]
            lines = jnp.where(wide == s + 1, line, lines)
        out[2 * EDGE :, :COLS] = lines


def bands_to_send(own, far, own_left, own_right, from_right, from_left, ions):
    whole = pl.BlockSpec((2, BAND, COLS), lambda i: (0, 0, 0))
    strip = pl.BlockSpec((STRIP, LANES), lambda i: (0, 0))
    shape = jax.ShapeDtypeStruct((BAND, COLS + LANES), jnp.float32)
    return pl.pallas_call(
        band_kernel,
        grid=(1,),
        in_specs=[
            whole,
            whole,
            strip,
            strip,
            strip,
            strip,
            pl.BlockSpec((3, 8, COLS), lambda i: (0, 0, 0)),
            pl.BlockSpec((3, 8, COLS), lambda i: (0, ROWS // 8 - 1, 0)),
        ],
        out_specs=[pl.BlockSpec((BAND, COLS + LANES), lambda i: (0, 0))] * 2,
        out_shape=[shape, shape],
        name="lat_bands",
    )(own, far, own_left, own_right, from_right, from_left, ions, ions)


def solve_kernel(
    factors, band, top, bottom, above, below, own_middle, far_middle,
    own_left, own_right, from_right, from_left,
    potential, drift_east, drift_north, fastest,
    sigma, sigma_next, sigma_prev, half_inverse, scaled_source, update, field, carried,
):
    theta = 0.5 * (HIGH_BOUND + LOW_BOUND)
    count = TILES + 1
    spans = [slice(t * LANES, (t + 1) * LANES) for t in range(count)]
    middle = slice(EDGE, ROWS - EDGE)

    for t in range(count):
        for piece, at in ((above, 0), (top, EDGE), (bottom, EDGE + ROWS - EDGE), (below, EDGE + ROWS)):
            sigma[t, at : at + EDGE] = piece[:EDGE, spans[t]]
            scaled_source[t, at : at + EDGE] = piece[EDGE : 2 * EDGE, spans[t]]
        inner = slice(2 * EDGE, 2 * EDGE + MID)
        if t < TILES:
            sigma[t, inner] = own_middle[0, :, spans[t]] + far_middle[0, :, spans[t]]
            source = own_middle[1, :, spans[t]] + far_middle[1, :, spans[t]]
            if t == 0:
                source = source + first_fix(from_left[middle])
            if t == TILES - 1:
                source = source + last_fix(from_right[middle])
        else:
            sigma[t, inner] = halo_sigma(from_right[middle], from_left[middle])
            source = halo_source(
                from_right[middle], from_left[middle], own_left[middle], own_right[middle]
            )
        scaled_source[t, inner] = source
        line = slice(2 * EDGE, 2 * EDGE + 1)
        row = row_index(8)
        tile = scaled_source[t, EDGE - 8 : EDGE]
        scaled_source[t, EDGE - 8 : EDGE] = tile + jnp.where(row == 7, 0.5 * top[line, spans[t]], 0.0)
        tile = scaled_source[t, EDGE : EDGE + 8]
        scaled_source[t, EDGE : EDGE + 8] = tile - jnp.where(row == 0, 0.5 * above[line, spans[t]], 0.0)
        low = EDGE + ROWS
        tile = scaled_source[t, low - 8 : low]
        scaled_source[t, low - 8 : low] = tile + jnp.where(row == 7, 0.5 * below[line, spans[t]], 0.0)
        tile = scaled_source[t, low : low + 8]
        scaled_source[t, low : low + 8] = tile - jnp.where(row == 0, 0.5 * bottom[line, spans[t]], 0.0)

    first_band = band[0] == 0
    last_band = band[0] == band[1] - 1
    blank = jnp.zeros((8, LANES), jnp.float32)
    for t in range(count):
        for slot in range(2):
            for at in (0, EXT - 8):
                field[slot, t, at : at + 8] = blank
                carried[slot, t, at : at + 8] = blank

    for start in range(8, EXT - 8, 8):
        here = [sigma[t, start : start + 8] for t in range(count)]
        sides = [sigma[t, start - 1 : start + 7] + sigma[t, start + 1 : start + 9] for t in range(count)]
        tall = [here[t] + 0.5 * sides[t] for t in range(count)]
        left = shifted(tall, True)
        right = shifted(tall, False)
        following = shifted(here, False)
        preceding = shifted(here, True)
        outside = None
        if start < EDGE:
            outside = first_band
        if start >= EDGE + ROWS:
            outside = last_band
        for t in range(count):
            diagonal = 0.5 * (6.0 * here[t] + (sides[t] + (left[t] + right[t]))) + DAMPING
            inverse = 1.0 / diagonal
            if outside is not None:
                inverse = jnp.where(outside, 0.0, inverse)
            source = scaled_source[t, start : start + 8] * inverse
            initial = source * (1.0 / theta)
            sigma_next[t, start : start + 8] = following[t]
            sigma_prev[t, start : start + 8] = preceding[t]
            half_inverse[t, start : start + 8] = 0.5 * inverse
            scaled_source[t, start : start + 8] = source
            update[t, start : start + 8] = initial
            field[1, t, start : start + 8] = initial
            carried[1, t, start : start + 8] = here[t] * initial

    def sweep(k, low, high):
        now = lax.rem(k, 2)
        later = 1 - now
        keep = factors[0, k - 1]
        gain = factors[1, k - 1]
        for start in range(low, high, 8):
            rows = slice(start, start + 8)
            upper = slice(start - 1, start + 7)
            lower = slice(start + 1, start + 9)
            centre, eastward, westward = ([], [], [])
            for t in range(count):
                value = field[now, t, rows]
                flux = carried[now, t, rows]
                value_sides = field[now, t, upper] + field[now, t, lower]
                flux_sides = carried[now, t, upper] + carried[now, t, lower]
                tall = value + 0.5 * value_sides
                flux_tall = flux + 0.5 * flux_sides
                centre.append(sigma[t, rows] * value_sides + flux_sides)
                eastward.append(sigma_next[t, rows] * tall + flux_tall)
                westward.append(sigma_prev[t, rows] * tall + flux_tall)
            from_west = shifted(eastward, True)
            from_east = shifted(westward, False)
            for t in range(count):
                total = centre[t] + (from_west[t] + from_east[t])
                value = field[now, t, rows]
                residual = (scaled_source[t, rows] - value) + half_inverse[t, rows] * total
                step = keep * update[t, rows] + gain * residual
                update[t, rows] = step
                value = value + step
                field[later, t, rows] = value
                carried[later, t, rows] = sigma[t, rows] * value

    def early(k, _):
        sweep(k, 8, EXT - 8)
        return 0

    def late(k, _):
        sweep(k, 16, EXT - 16)
        return 0

    lax.fori_loop(1, 8, early, 0)
    lax.fori_loop(8, SWEEPS, late, 0)

    last = SWEEPS % 2
    top_speed = jnp.zeros((8, LANES), jnp.float32)
    for start in range(EDGE, EDGE + ROWS, 8):
        rows = slice(start, start + 8)
        out = slice(start - EDGE, start - EDGE + 8)
        tiles = [field[last, t, rows] for t in range(count)]
        west = shifted(tiles, True)
        east = shifted(tiles, False)
        for t in range(TILES):
            potential[out, spans[t]] = tiles[t]
            lift = -0.5 * (field[last, t, start + 1 : start + 9] - field[last, t, start - 1 : start + 7])
            shove = 0.5 * (east[t] - west[t])
            drift_east[out, spans[t]] = lift
            drift_north[out, spans[t]] = shove
            top_speed = jnp.maximum(top_speed, jnp.abs(lift) + jnp.abs(shove))
    peak = jnp.max(top_speed, axis=1, keepdims=True)
    peak = jnp.max(peak, axis=0, keepdims=True)
    fastest[...] = jnp.broadcast_to(peak[None], fastest.shape)


def solve(peers, factors, band, *fields):
    shapes = [(ROWS, COLS)] * 3 + [(peers, 1, LANES)]
    plane = (TILES + 1, EXT, LANES)
    memory = pltpu.VMEM(plane, jnp.float32)
    pair = pltpu.VMEM((2,) + plane, jnp.float32)
    return pl.pallas_call(
        solve_kernel,
        in_specs=[pl.BlockSpec(memory_space=pltpu.SMEM)] * 2
        + [pl.BlockSpec(memory_space=pltpu.VMEM)] * len(fields),
        out_specs=[pl.BlockSpec(memory_space=pltpu.VMEM)] * 4,
        out_shape=[jax.ShapeDtypeStruct(shape, jnp.float32) for shape in shapes],
        scratch_shapes=[memory] * 6 + [pair] * 2,
        compiler_params=pltpu.CompilerParams(vmem_limit_bytes=VMEM_BYTES),
        name="potential_solve",
    )(factors, band, *fields)


def advect_kernel(fastest, drift_east, drift_north, ions, above, below, from_right, from_left, out):
    peak = jnp.max(fastest[...], axis=0)
    peak = jnp.max(peak, axis=1, keepdims=True)
    time_step = COURANT / (peak + 1e-06)
    lane = lane_index(ROWS)
    wide = row_index(ROWS, LANES)
    for s in range(3):
        pace = MOBILITY[s] * time_step
        tiles = [ions[s, :, t * LANES : (t + 1) * LANES] for t in range(TILES)]
        left = [pltpu.roll(tile, 1, 1) for tile in tiles]
        right = [pltpu.roll(tile, LANES - 1, 1) for tile in tiles]
        edge_right = pltpu.roll(from_right[:ROWS], SIDE * 2 - 1 - s, 1)
        edge_left = pltpu.roll(from_left[:ROWS], LANES - SIDE - s, 1)
        for t in range(TILES):
            span = slice(t * LANES, (t + 1) * LANES)
            density = tiles[t]
            west = jnp.where(lane == 0, left[t - 1] if t else edge_left, left[t])
            east = jnp.where(lane == LANES - 1, right[t + 1] if t < TILES - 1 else edge_right, right[t])
            line = slice(2 * EDGE + 1 + s, 2 * EDGE + 2 + s)
            south = jnp.where(wide == 0, above[line, span], pltpu.roll(density, 1, 0))
            north = jnp.where(wide == ROWS - 1, below[line, span], pltpu.roll(density, ROWS - 1, 0))
            cross_east = pace * drift_east[:, span]
            cross_north = pace * drift_north[:, span]
            result = density - jnp.maximum(cross_east, 0.0) * (density - west)
            result = result - jnp.minimum(cross_east, 0.0) * (east - density)
            result = result - jnp.maximum(cross_north, 0.0) * (density - south)
            result = result - jnp.minimum(cross_north, 0.0) * (north - density)
            out[s, :, span] = result


def advect(*fields):
    return pl.pallas_call(
        advect_kernel,
        in_specs=[pl.BlockSpec(memory_space=pltpu.VMEM)] * len(fields),
        out_specs=pl.BlockSpec(memory_space=pltpu.VMEM),
        out_shape=jax.ShapeDtypeStruct((3, ROWS, COLS), jnp.float32),
        compiler_params=pltpu.CompilerParams(vmem_limit_bytes=VMEM_BYTES),
        name="ion_advection",
    )(*fields)


def shards(pedersen, hall_conductivity, east_wind, north_wind, ion_density):
    lats = lax.axis_size("lat")
    lons = lax.axis_size("lon")
    mirror = [(i, lats - 1 - i) for i in range(lats)]
    eastward = [(i, (i + 1) % lons) for i in range(lons)]
    westward = [(j, i) for i, j in eastward]
    rising = [(i, i + 1) for i in range(lats - 1)]
    falling = [(j, i) for i, j in rising]

    own_strips, own_bands, own_middle, strips, bands, middle = column_sums(
        pedersen, hall_conductivity, east_wind, north_wind
    )
    far_strips = lax.ppermute(strips, "lat", mirror)
    far_bands = lax.ppermute(bands, "lat", mirror)
    far_middle = lax.ppermute(middle, "lat", mirror)
    to_left, to_right = strips_to_send(own_strips, far_strips, ion_density)
    from_right = lax.ppermute(to_left, "lon", westward)
    from_left = lax.ppermute(to_right, "lon", eastward)
    top, bottom = bands_to_send(
        own_bands, far_bands, to_left, to_right, from_right, from_left, ion_density
    )
    above = lax.ppermute(bottom, "lat", rising)
    below = lax.ppermute(top, "lat", falling)

    theta, first_list, second_list = chebyshev_factors()
    factors = jnp.array([first_list, second_list], jnp.float32)
    band = jnp.stack([lax.axis_index("lat").astype(jnp.int32), jnp.int32(lats)])
    potential, drift_east, drift_north, peaks = solve(
        lats * lons, factors, band, top, bottom, above, below, own_middle, far_middle,
        to_left, to_right, from_right, from_left,
    )
    peaks = lax.all_to_all(peaks, ("lat", "lon"), 0, 0, tiled=True)
    ion_update = advect(
        peaks, drift_east, drift_north, ion_density, above, below, from_right, from_left
    )
    return (potential, ion_update)


def solution(mesh):
    spec = P(None, "lat", "lon")
    return jax.shard_map(
        shards,
        mesh=mesh,
        in_specs=(spec,) * 5,
        out_specs=(P("lat", "lon"), spec),
        check_vma=False,
    )
```

```python
import functools

import jax
import jax.numpy as jnp
from jax import lax
from jax.experimental import pallas as pl
from jax.experimental.pallas import tpu as pltpu
from jax.sharding import PartitionSpec as P

LEV = 16
SWEEPS = 16
DAMPING = 0.0001
LOW_BOUND = 0.05
HIGH_BOUND = 2.0
COURANT = 0.8
MOBILITY = (1.0, 0.6, 0.3)

LANES = 128
ROWS = 128
COLS = 512
TILES = COLS // LANES
WIDE = COLS + LANES
EDGE = 16
HALO = 24
MID = ROWS - 2 * EDGE
EXT = ROWS + 2 * HALO
SIGMA_PLUS = 2 * EDGE
CURRENT = SIGMA_PLUS + 1
IONS = SIGMA_PLUS + 2
NORTH = SIGMA_PLUS + 5
LINES = SIGMA_PLUS + 8
CHUNK = 16
VMEM_BYTES = 32 * 1024 * 1024


def chebyshev_factors():
    theta = 0.5 * (HIGH_BOUND + LOW_BOUND)
    delta = 0.5 * (HIGH_BOUND - LOW_BOUND)
    sigma_one = theta / delta
    rho_prev = 1.0 / sigma_one
    first_list = []
    second_list = []
    for sweep in range(SWEEPS):
        rho_next = 1.0 / (2.0 * sigma_one - rho_prev)
        first_list.append(rho_next * rho_prev)
        second_list.append(2.0 * rho_next / delta)
        rho_prev = rho_next
    return (theta, first_list, second_list)


def in_vmem(kernel, name, shapes, *fields):
    whole = pl.BlockSpec(memory_space=pltpu.VMEM)
    return pl.pallas_call(
        kernel,
        in_specs=[whole] * len(fields),
        out_specs=jax.tree.map(lambda _: whole, shapes),
        out_shape=shapes,
        compiler_params=pltpu.CompilerParams(vmem_limit_bytes=VMEM_BYTES),
        name=name,
    )(*fields)


def lane_index(rows):
    return lax.broadcasted_iota(jnp.int32, (rows, LANES), 1)


def row_index(rows, cols=LANES):
    return lax.broadcasted_iota(jnp.int32, (rows, cols), 0)


def reversed_rows(tile):
    row = row_index(8, tile.shape[1])
    tile = pltpu.roll(tile, 4, 0)
    tile = jnp.where((row & 2) == 0, pltpu.roll(tile, 6, 0), pltpu.roll(tile, 2, 0))
    return jnp.where((row & 1) == 0, pltpu.roll(tile, 7, 0), pltpu.roll(tile, 1, 0))


def shifted(tiles, to_right):
    count = len(tiles)
    lane = lane_index(tiles[0].shape[0])
    if to_right:
        turned = [pltpu.roll(tile, 1, 1) for tile in tiles]
        return [jnp.where(lane == 0, turned[t - 1], turned[t]) for t in range(count)]
    turned = [pltpu.roll(tile, LANES - 1, 1) for tile in tiles]
    return [jnp.where(lane == LANES - 1, turned[(t + 1) % count], turned[t]) for t in range(count)]


def local_source(east, north, source, start, rows):
    tiles = [east[start : start + rows, t * LANES : (t + 1) * LANES] for t in range(TILES)]
    lane = lane_index(rows)
    row = row_index(rows)
    left = [pltpu.roll(tile, 1, 1) for tile in tiles]
    right = [pltpu.roll(tile, LANES - 1, 1) for tile in tiles]
    zero = jnp.zeros((rows, LANES), jnp.float32)
    for t in range(TILES):
        span = slice(t * LANES, (t + 1) * LANES)
        before = jnp.where(lane == 0, left[t - 1] if t else zero, left[t])
        after = jnp.where(lane == LANES - 1, right[t + 1] if t < TILES - 1 else zero, right[t])
        here = north[start : start + rows, span]
        up = pltpu.roll(here, 1, 0)
        down = pltpu.roll(here, rows - 1, 0)
        above = north[start - 8 : start, span][7:8] if start else zero[:1]
        below = north[start + rows : start + rows + 8, span][:1] if start + rows < ROWS else zero[:1]
        up = jnp.where(row == 0, above, up)
        down = jnp.where(row == rows - 1, below, down)
        source[start : start + rows, span] = 0.5 * (after - before) + 0.5 * (down - up)


def put_lanes(tile, source, at, first, count):
    lane = lane_index(tile.shape[0])
    turn = (first - at) % LANES
    moved = pltpu.roll(source, turn, 1) if turn else source
    return jnp.where((lane >= first) & (lane < first + count), moved, tile)


def write_pieces(sigma, east, north, source, edges, middle):
    for start in range(0, ROWS, 8):
        local_source(east, north, source, start, 8)
    row = row_index(8)
    wide = row_index(8, COLS)
    for side in range(2):
        at = side * (COLS - LANES)
        span = slice(at, at + LANES)
        near = side * (LANES - EDGE)
        strip = jnp.zeros((ROWS, LANES), jnp.float32)
        strip = put_lanes(strip, sigma[:, span], near, 0, EDGE)
        strip = put_lanes(strip, source[:, span], near, EDGE, EDGE)
        strip = put_lanes(strip, sigma[:, span], LANES - EDGE - 1 if side else EDGE, SIGMA_PLUS, 1)
        strip = put_lanes(strip, east[:, span], side * (LANES - 1), CURRENT, 1)
        turned = strip.T
        edges[side, :SIGMA_PLUS, COLS:] = turned[:SIGMA_PLUS]
        tile = turned[SIGMA_PLUS:LINES]
        tile = jnp.where(row == NORTH - SIGMA_PLUS, north[0:8, span][:1], tile)
        tile = jnp.where(row == NORTH + 1 - SIGMA_PLUS, north[ROWS - 8 :, span][7:8], tile)
        edges[side, SIGMA_PLUS:, COLS:] = tile
        first = side * (ROWS - EDGE)
        edges[side, :EDGE, :COLS] = sigma[first : first + EDGE]
        edges[side, EDGE : 2 * EDGE, :COLS] = source[first : first + EDGE]
        if side == 0:
            further, line = (sigma[EDGE : EDGE + 8][:1], north[0:8][:1])
        else:
            further, line = (sigma[first - 8 : first][7:8], north[ROWS - 8 :][7:8])
        tile = jnp.where(wide == 0, further, 0.0)
        edges[side, SIGMA_PLUS:, :COLS] = jnp.where(wide == 1, line, tile)
    middle[0] = sigma[EDGE : ROWS - EDGE]
    middle[1] = source[EDGE : ROWS - EDGE]


def column_kernel(
    pedersen, hall, east_wind, north_wind,
    own_edges, own_middle, far_edges, far_middle,
    held, sigma, east, north, sigma_far, east_far, north_far, source, arrived,
):
    steps = ROWS // CHUNK

    def copies(step):
        rows = pl.ds(pl.multiple_of(step * CHUNK, CHUNK), CHUNK)
        return [
            pltpu.make_async_copy(field.at[:, rows, :], held.at[i, :, rows, :], arrived.at[i, step])
            for i, field in enumerate((pedersen, hall, east_wind, north_wind))
        ]

    for step in range(steps):
        for copy in copies(step):
            copy.start()

    def body(step, _):
        for copy in copies(step):
            copy.wait()
        for half in range(CHUNK // 8):
            near = pl.ds(pl.multiple_of(step * CHUNK + half * 8, 8), 8)
            away = pl.ds(pl.multiple_of(ROWS - 8 - step * CHUNK - half * 8, 8), 8)
            totals = [jnp.zeros((8, COLS), jnp.float32) for _ in range(3)]
            for level in range(LEV):
                layer = (0.5 + level / LEV) / LEV
                along = layer * held[0, level, near, :]
                across = layer * held[1, level, near, :]
                wind_e = held[2, level, near, :]
                wind_n = held[3, level, near, :]
                totals[0] = totals[0] + along
                totals[1] = totals[1] + (along * wind_e + across * wind_n)
                totals[2] = totals[2] + (along * wind_n - across * wind_e)
            pairs = zip(totals, (sigma, east, north), (sigma_far, east_far, north_far))
            for total, here, there in pairs:
                here[near, :] = total
                there[away, :] = reversed_rows(total)
        return 0

    lax.fori_loop(0, steps, body, 0)
    write_pieces(sigma_far, east_far, north_far, source, far_edges, far_middle)
    write_pieces(sigma, east, north, source, own_edges, own_middle)


def column_sums(*levels):
    shapes = [(2, LINES, WIDE), (2, MID, COLS)] * 2
    field = pltpu.VMEM((ROWS, COLS), jnp.float32)
    return pl.pallas_call(
        column_kernel,
        in_specs=[pl.BlockSpec(memory_space=pltpu.HBM)] * 4,
        out_specs=[pl.BlockSpec(memory_space=pltpu.VMEM)] * 4,
        out_shape=[jax.ShapeDtypeStruct(shape, jnp.float32) for shape in shapes],
        scratch_shapes=[pltpu.VMEM((4, LEV, ROWS, COLS), jnp.float32)]
        + [field] * 7
        + [pltpu.SemaphoreType.DMA((4, ROWS // CHUNK))],
        compiler_params=pltpu.CompilerParams(vmem_limit_bytes=VMEM_BYTES),
        name="column_sums",
    )(*levels)


def ion_kernel(ions, out):
    row = row_index(8)
    for side in range(2):
        at = side * (COLS - LANES)
        tile = jnp.zeros((8, LANES), jnp.float32)
        for s in range(3):
            turned = ions[s, :, at : at + LANES].T
            line = turned[LANES - 1 :] if side else turned[:1]
            tile = jnp.where(row == IONS - SIGMA_PLUS + s, line, tile)
        out[side] = tile


def ion_columns(ions):
    shape = jax.ShapeDtypeStruct((2, 8, LANES), jnp.float32)
    return in_vmem(ion_kernel, "ion_columns", shape, ions)


def strip_kernel(own, far, ion_lines, to_left, to_right):
    for side, out in ((0, to_left), (1, to_right)):
        total = own[side, :, COLS:] + far[side, :, COLS:]
        out[:SIGMA_PLUS] = total[:SIGMA_PLUS]
        out[SIGMA_PLUS:] = total[SIGMA_PLUS:] + ion_lines[side]


def strips_to_send(*fields):
    shape = jax.ShapeDtypeStruct((LINES, LANES), jnp.float32)
    return in_vmem(strip_kernel, "lon_strips", [shape, shape], *fields)


def turned_back(strip):
    rest = jnp.zeros((LANES - LINES, LANES), jnp.float32)
    return jnp.concatenate([strip[...], rest], 0).T


def band_kernel(own, far, own_left, own_right, from_right, from_left, ions, top, bottom, beside):
    right, left = (turned_back(from_right), turned_back(from_left))
    ours_right, ours_left = (turned_back(own_right), turned_back(own_left))
    blank = jnp.zeros((ROWS, LANES), jnp.float32)
    sigma = put_lanes(blank, right, 0, 0, EDGE)
    sigma = put_lanes(sigma, right, SIGMA_PLUS, EDGE, 1)
    sigma = put_lanes(sigma, left, 0, LANES - EDGE, EDGE)
    sigma = put_lanes(sigma, left, SIGMA_PLUS, LANES - EDGE - 1, 1)
    source = put_lanes(blank, right, EDGE, 0, EDGE)
    source = put_lanes(source, left, EDGE, LANES - EDGE, EDGE)
    source = source - 0.5 * put_lanes(blank, ours_right, CURRENT, 0, 1)
    source = source + 0.5 * put_lanes(blank, ours_left, CURRENT, LANES - 1, 1)
    mend = put_lanes(blank, -0.5 * left, CURRENT, 0, 1)
    mend = put_lanes(mend, 0.5 * right, CURRENT, LANES - 1, 1)
    beside[0] = sigma
    beside[1] = source
    beside[2] = mend

    part = slice(EDGE, 2 * EDGE)
    lane = lane_index(EDGE)
    row = row_index(8)
    wide = row_index(8, COLS)
    for side, out in ((0, top), (1, bottom)):
        first = side * (ROWS - EDGE)
        rows = slice(first, first + EDGE)
        out[:SIGMA_PLUS, :COLS] = own[side, :SIGMA_PLUS, :COLS] + far[side, :SIGMA_PLUS, :COLS]
        out[part, :LANES] += jnp.where(lane == 0, mend[rows], 0.0)
        out[part, COLS - LANES : COLS] += jnp.where(lane == LANES - 1, mend[rows], 0.0)
        lines = own[side, SIGMA_PLUS:, :COLS] + far[side, SIGMA_PLUS:, :COLS]
        for s in range(3):
            line = ions[s, ROWS - 8 :][7:8] if side else ions[s, :8][:1]
            lines = jnp.where(wide == IONS - SIGMA_PLUS + s, line, lines)
        out[SIGMA_PLUS:, :COLS] = lines
        out[:EDGE, COLS:] = sigma[rows]
        out[part, COLS:] = source[rows]
        further = sigma[first - 1 : first] if side else sigma[EDGE : EDGE + 1]
        north = jnp.where(
            lane[:1] < LANES // 2,
            from_right[SIGMA_PLUS:][NORTH - SIGMA_PLUS + side :][:1],
            from_left[SIGMA_PLUS:][NORTH - SIGMA_PLUS + side :][:1],
        )
        tile = jnp.where(row == 0, further, 0.0)
        out[SIGMA_PLUS:, COLS:] = jnp.where(row == CURRENT - SIGMA_PLUS, north, tile)


def bands_to_send(*fields):
    shape = jax.ShapeDtypeStruct((LINES, WIDE), jnp.float32)
    beside = jax.ShapeDtypeStruct((3, ROWS, LANES), jnp.float32)
    return in_vmem(band_kernel, "lat_bands", [shape, shape, beside], *fields)


def solve_kernel(
    factors, band, top, bottom, beside, above, below, own_middle, far_middle,
    potential, drift_east, drift_north, fastest,
    sigma, sigma_next, sigma_prev, half_inverse, scaled_source, update, field_a, field_b, carried_a, carried_b,
):
    theta = 0.5 * (HIGH_BOUND + LOW_BOUND)
    fields = (field_a, field_b)
    fluxes = (carried_a, carried_b)
    count = TILES + 1
    spans = [slice(t * LANES, (t + 1) * LANES) for t in range(count)]
    middle = slice(EDGE, ROWS - EDGE)
    row = row_index(8)
    low = HALO + ROWS

    for t in range(count):
        span = spans[t]
        for piece, at in ((above, HALO - EDGE), (top, HALO), (bottom, low - EDGE), (below, low)):
            sigma[t, at : at + EDGE] = piece[:EDGE, span]
            scaled_source[t, at : at + EDGE] = piece[EDGE : 2 * EDGE, span]
        outer = above[SIGMA_PLUS:, span][:1]
        sigma[t, :8] = jnp.where(row == 7, outer, 0.0)
        outer = below[SIGMA_PLUS:, span][:1]
        sigma[t, EXT - 8 :] = jnp.where(row == 0, outer, 0.0)
        inner = slice(HALO + EDGE, low - EDGE)
        if t < TILES:
            sigma[t, inner] = own_middle[0, :, span] + far_middle[0, :, span]
            source = own_middle[1, :, span] + far_middle[1, :, span]
            lane = lane_index(MID)
            if t == 0:
                source = source + jnp.where(lane == 0, beside[2, middle], 0.0)
            if t == TILES - 1:
                source = source + jnp.where(lane == LANES - 1, beside[2, middle], 0.0)
        else:
            sigma[t, inner] = beside[0, middle]
            source = beside[1, middle]
        scaled_source[t, inner] = source
        for at, spot, piece, half in (
            (HALO - 8, 7, top, 0.5),
            (HALO, 0, above, -0.5),
            (low - 8, 7, below, 0.5),
            (low, 0, bottom, -0.5),
        ):
            line = half * piece[SIGMA_PLUS:, span][CURRENT - SIGMA_PLUS :][:1]
            tile = scaled_source[t, at : at + 8]
            scaled_source[t, at : at + 8] = tile + jnp.where(row == spot, line, 0.0)

    first_band = band[0] == 0
    last_band = band[0] == band[1] - 1
    blank = jnp.zeros((8, LANES), jnp.float32)
    for t in range(count):
        for slot in range(2):
            for at in (0, EXT - 8):
                fields[slot][t, at : at + 8] = blank
                fluxes[slot][t, at : at + 8] = blank

    for start in range(8, EXT - 8, 8):
        here = [sigma[t, start : start + 8] for t in range(count)]
        sides = [sigma[t, start - 1 : start + 7] + sigma[t, start + 1 : start + 9] for t in range(count)]
        tall = [here[t] + 0.5 * sides[t] for t in range(count)]
        left = shifted(tall, True)
        right = shifted(tall, False)
        following = shifted(here, False)
        preceding = shifted(here, True)
        outside = None
        if start < HALO:
            outside = first_band
        if start >= HALO + ROWS:
            outside = last_band
        for t in range(count):
            diagonal = 0.5 * (6.0 * here[t] + (sides[t] + (left[t] + right[t]))) + DAMPING
            inverse = 1.0 / diagonal
            if outside is not None:
                inverse = jnp.where(outside, 0.0, inverse)
            source = scaled_source[t, start : start + 8] * inverse
            initial = source * (1.0 / theta)
            sigma_next[t, start : start + 8] = following[t]
            sigma_prev[t, start : start + 8] = preceding[t]
            half_inverse[t, start : start + 8] = 0.5 * inverse
            scaled_source[t, start : start + 8] = source
            update[t, start : start + 8] = initial
            field_b[t, start : start + 8] = initial
            carried_b[t, start : start + 8] = here[t] * initial

    def sweep(k, now, later, low, high):
        field_now, carried_now = (fields[now], fluxes[now])
        field_later, carried_later = (fields[later], fluxes[later])
        keep = factors[0, k - 1]
        gain = factors[1, k - 1]
        for start in range(low, high, 8):
            rows = slice(start, start + 8)
            upper = slice(start - 1, start + 7)
            lower = slice(start + 1, start + 9)
            centre, eastward, westward = ([], [], [])
            for t in range(count):
                value = field_now[t, rows]
                flux = carried_now[t, rows]
                value_sides = field_now[t, upper] + field_now[t, lower]
                flux_sides = carried_now[t, upper] + carried_now[t, lower]
                tall = value + 0.5 * value_sides
                flux_tall = flux + 0.5 * flux_sides
                centre.append(sigma[t, rows] * value_sides + flux_sides)
                eastward.append(sigma_next[t, rows] * tall + flux_tall)
                westward.append(sigma_prev[t, rows] * tall + flux_tall)
            from_west = shifted(eastward, True)
            from_east = shifted(westward, False)
            for t in range(count):
                total = centre[t] + (from_west[t] + from_east[t])
                value = field_now[t, rows]
                residual = (scaled_source[t, rows] - value) + half_inverse[t, rows] * total
                step = keep * update[t, rows] + gain * residual
                update[t, rows] = step
                value = value + step
                field_later[t, rows] = value
                carried_later[t, rows] = sigma[t, rows] * value

    def early(pair, _):
        sweep(2 * pair + 1, 1, 0, 8, EXT - 8)
        sweep(2 * pair + 2, 0, 1, 8, EXT - 8)
        return 0

    def late(pair, _):
        sweep(2 * pair + 9, 1, 0, 16, EXT - 16)
        sweep(2 * pair + 10, 0, 1, 16, EXT - 16)
        return 0

    lax.fori_loop(0, 4, early, 0)
    lax.fori_loop(0, 3, late, 0)
    sweep(15, 1, 0, 16, EXT - 16)

    last = fields[SWEEPS % 2]
    top_speed = jnp.zeros((8, LANES), jnp.float32)
    for start in range(HALO, HALO + ROWS, 8):
        rows = slice(start, start + 8)
        out = slice(start - HALO, start - HALO + 8)
        tiles = [last[t, rows] for t in range(count)]
        west = shifted(tiles, True)
        east = shifted(tiles, False)
        for t in range(TILES):
            potential[out, spans[t]] = tiles[t]
            lift = -0.5 * (last[t, start + 1 : start + 9] - last[t, start - 1 : start + 7])
            shove = 0.5 * (east[t] - west[t])
            drift_east[out, spans[t]] = lift
            drift_north[out, spans[t]] = shove
            top_speed = jnp.maximum(top_speed, jnp.abs(lift) + jnp.abs(shove))
    peak = jnp.max(top_speed, axis=1, keepdims=True)
    peak = jnp.max(peak, axis=0, keepdims=True)
    fastest[...] = jnp.broadcast_to(peak[None], fastest.shape)


def solve(peers, factors, band, *fields):
    shapes = [(ROWS, COLS)] * 3 + [(peers, 1, LANES)]
    plane = (TILES + 1, EXT, LANES)
    memory = pltpu.VMEM(plane, jnp.float32)
    return pl.pallas_call(
        solve_kernel,
        in_specs=[pl.BlockSpec(memory_space=pltpu.SMEM)] * 2
        + [pl.BlockSpec(memory_space=pltpu.VMEM)] * len(fields),
        out_specs=[pl.BlockSpec(memory_space=pltpu.VMEM)] * 4,
        out_shape=[jax.ShapeDtypeStruct(shape, jnp.float32) for shape in shapes],
        scratch_shapes=[memory] * 10,
        compiler_params=pltpu.CompilerParams(vmem_limit_bytes=VMEM_BYTES),
        name="potential_solve",
    )(factors, band, *fields)


def advect_kernel(fastest, drift_east, drift_north, ions, above, below, from_right, from_left, out):
    peak = jnp.max(fastest[...], axis=0)
    peak = jnp.max(peak, axis=1, keepdims=True)
    time_step = COURANT / (peak + 1e-06)
    lane = lane_index(ROWS)
    wide = row_index(ROWS, LANES)
    beyond_right, beyond_left = (turned_back(from_right), turned_back(from_left))
    for s in range(3):
        pace = MOBILITY[s] * time_step
        tiles = [ions[s, :, t * LANES : (t + 1) * LANES] for t in range(TILES)]
        left = [pltpu.roll(tile, 1, 1) for tile in tiles]
        right = [pltpu.roll(tile, LANES - 1, 1) for tile in tiles]
        edge_right = pltpu.roll(beyond_right, LANES - 1 - IONS - s, 1)
        edge_left = pltpu.roll(beyond_left, LANES - IONS - s, 1)
        for t in range(TILES):
            span = slice(t * LANES, (t + 1) * LANES)
            density = tiles[t]
            west = jnp.where(lane == 0, left[t - 1] if t else edge_left, left[t])
            east = jnp.where(lane == LANES - 1, right[t + 1] if t < TILES - 1 else edge_right, right[t])
            behind = above[SIGMA_PLUS:, span][IONS - SIGMA_PLUS + s :][:1]
            ahead = below[SIGMA_PLUS:, span][IONS - SIGMA_PLUS + s :][:1]
            south = jnp.where(wide == 0, behind, pltpu.roll(density, 1, 0))
            north = jnp.where(wide == ROWS - 1, ahead, pltpu.roll(density, ROWS - 1, 0))
            cross_east = pace * drift_east[:, span]
            cross_north = pace * drift_north[:, span]
            result = density - jnp.maximum(cross_east, 0.0) * (density - west)
            result = result - jnp.minimum(cross_east, 0.0) * (east - density)
            result = result - jnp.maximum(cross_north, 0.0) * (density - south)
            result = result - jnp.minimum(cross_north, 0.0) * (north - density)
            out[s, :, span] = result


def advect(*fields):
    shape = jax.ShapeDtypeStruct((3, ROWS, COLS), jnp.float32)
    return in_vmem(advect_kernel, "ion_advection", shape, *fields)


def shards(pedersen, hall_conductivity, east_wind, north_wind, ion_density):
    lats = lax.axis_size("lat")
    lons = lax.axis_size("lon")
    mirror = [(i, lats - 1 - i) for i in range(lats)]
    eastward = [(i, (i + 1) % lons) for i in range(lons)]
    westward = [(j, i) for i, j in eastward]
    rising = [(i, i + 1) for i in range(lats - 1)]
    falling = [(j, i) for i, j in rising]

    own_edges, own_middle, edges, middle = column_sums(
        pedersen, hall_conductivity, east_wind, north_wind
    )
    far_edges = lax.ppermute(edges, "lat", mirror)
    far_middle = lax.ppermute(middle, "lat", mirror)
    ion_lines = ion_columns(ion_density)
    to_left, to_right = strips_to_send(own_edges, far_edges, ion_lines)
    from_right = lax.ppermute(to_left, "lon", westward)
    from_left = lax.ppermute(to_right, "lon", eastward)
    top, bottom, beside = bands_to_send(
        own_edges, far_edges, to_left, to_right, from_right, from_left, ion_density
    )
    above = lax.ppermute(bottom, "lat", rising)
    below = lax.ppermute(top, "lat", falling)

    theta, first_list, second_list = chebyshev_factors()
    factors = jnp.array([first_list, second_list], jnp.float32)
    band = jnp.stack([lax.axis_index("lat").astype(jnp.int32), jnp.int32(lats)])
    potential, drift_east, drift_north, peaks = solve(
        lats * lons, factors, band, top, bottom, beside, above, below, own_middle, far_middle
    )
    peaks = lax.all_to_all(peaks, ("lat", "lon"), 0, 0, tiled=True)
    ion_update = advect(
        peaks, drift_east, drift_north, ion_density, above, below, from_right, from_left
    )
    return (potential, ion_update)


def solution(mesh):
    spec = P(None, "lat", "lon")
    return jax.shard_map(
        shards,
        mesh=mesh,
        in_specs=(spec,) * 5,
        out_specs=(P("lat", "lon"), spec),
        check_vma=False,
    )
```

```python
import functools

import jax
import jax.numpy as jnp
from jax import lax
from jax.experimental import pallas as pl
from jax.experimental.pallas import tpu as pltpu
from jax.sharding import PartitionSpec as P

LEV = 16
SWEEPS = 16
DAMPING = 0.0001
LOW_BOUND = 0.05
HIGH_BOUND = 2.0
COURANT = 0.8
MOBILITY = (1.0, 0.6, 0.3)

LANES = 128
ROWS = 128
COLS = 512
TILES = COLS // LANES
WIDE = COLS + LANES
SEND = WIDE + LANES
PART = COLS // 2
EDGE = 16
HALO = 24
MID = ROWS - 2 * EDGE
EXT = ROWS + 2 * HALO
SIGMA_PLUS = 2 * EDGE
CURRENT = SIGMA_PLUS + 1
IONS = SIGMA_PLUS + 2
NORTH = SIGMA_PLUS + 5
LINES = SIGMA_PLUS + 8
CHUNK = 16
VMEM_BYTES = 32 * 1024 * 1024
COLUMN_BYTES = 51 * 1024 * 1024


def chebyshev_factors():
    theta = 0.5 * (HIGH_BOUND + LOW_BOUND)
    delta = 0.5 * (HIGH_BOUND - LOW_BOUND)
    sigma_one = theta / delta
    rho_prev = 1.0 / sigma_one
    first_list = []
    second_list = []
    for sweep in range(SWEEPS):
        rho_next = 1.0 / (2.0 * sigma_one - rho_prev)
        first_list.append(rho_next * rho_prev)
        second_list.append(2.0 * rho_next / delta)
        rho_prev = rho_next
    return (theta, first_list, second_list)


def lane_index(rows):
    return lax.broadcasted_iota(jnp.int32, (rows, LANES), 1)


def row_index(rows, cols=LANES):
    return lax.broadcasted_iota(jnp.int32, (rows, cols), 0)


def reversed_rows(tile):
    row = row_index(8, tile.shape[1])
    tile = pltpu.roll(tile, 4, 0)
    tile = jnp.where((row & 2) == 0, pltpu.roll(tile, 6, 0), pltpu.roll(tile, 2, 0))
    return jnp.where((row & 1) == 0, pltpu.roll(tile, 7, 0), pltpu.roll(tile, 1, 0))


def shifted(tiles, to_right):
    count = len(tiles)
    lane = lane_index(tiles[0].shape[0])
    if to_right:
        turned = [pltpu.roll(tile, 1, 1) for tile in tiles]
        return [jnp.where(lane == 0, turned[t - 1], turned[t]) for t in range(count)]
    turned = [pltpu.roll(tile, LANES - 1, 1) for tile in tiles]
    return [jnp.where(lane == LANES - 1, turned[(t + 1) % count], turned[t]) for t in range(count)]


def local_source(east, north, source, start, wanted):
    rows = slice(start, start + 8)
    lane = lane_index(8)
    row = row_index(8)
    zero = jnp.zeros((8, LANES), jnp.float32)
    tiles = east.shape[1] // LANES
    for t in wanted:
        span = slice(t * LANES, (t + 1) * LANES)
        tile = east[rows, span]
        left = right = zero
        if t:
            left = pltpu.roll(east[rows, (t - 1) * LANES : t * LANES], 1, 1)
        if t < tiles - 1:
            right = pltpu.roll(east[rows, (t + 1) * LANES : (t + 2) * LANES], LANES - 1, 1)
        before = jnp.where(lane == 0, left, pltpu.roll(tile, 1, 1))
        after = jnp.where(lane == LANES - 1, right, pltpu.roll(tile, LANES - 1, 1))
        here = north[rows, span]
        above = north[start - 8 : start, span][7:8] if start else zero[:1]
        below = north[start + 8 : start + 16, span][:1] if start + 8 < ROWS else zero[:1]
        up = jnp.where(row == 0, above, pltpu.roll(here, 1, 0))
        down = jnp.where(row == 7, below, pltpu.roll(here, 7, 0))
        source[rows, span] = 0.5 * (after - before) + 0.5 * (down - up)


def put_lanes(tile, source, at, first, count):
    lane = lane_index(tile.shape[0])
    turn = (first - at) % LANES
    moved = pltpu.roll(source, turn, 1) if turn else source
    return jnp.where((lane >= first) & (lane < first + count), moved, tile)


def write_strips(sums, ions, source, strips):
    sigma, east, north = (sums.at[0], sums.at[1], sums.at[2])
    for start in range(0, ROWS, 8):
        local_source(east, north, source, start, (0, 1))
    row = row_index(8)
    for side, out in enumerate(strips):
        span = slice(side * LANES, (side + 1) * LANES)
        near = side * (LANES - EDGE)
        strip = jnp.zeros((ROWS, LANES), jnp.float32)
        strip = put_lanes(strip, sigma[:, span], near, 0, EDGE)
        strip = put_lanes(strip, source[:, span], near, EDGE, EDGE)
        strip = put_lanes(strip, sigma[:, span], LANES - EDGE - 1 if side else EDGE, SIGMA_PLUS, 1)
        strip = put_lanes(strip, east[:, span], side * (LANES - 1), CURRENT, 1)
        if ions is not None:
            for s in range(3):
                strip = put_lanes(strip, ions[s, :, span], side * (LANES - 1), IONS + s, 1)
        turned = strip.T
        out[:SIGMA_PLUS] = turned[:SIGMA_PLUS]
        tile = turned[SIGMA_PLUS:LINES]
        tile = jnp.where(row == NORTH - SIGMA_PLUS, north[0:8, span][:1], tile)
        out[SIGMA_PLUS:] = jnp.where(row == NORTH + 1 - SIGMA_PLUS, north[ROWS - 8 :, span][7:8], tile)


def sum_levels(fields, spans, held, arrived, own, far, before=()):
    steps = ROWS // CHUNK

    def copies(step):
        rows = pl.ds(pl.multiple_of(step * CHUNK, CHUNK), CHUNK)
        out = []
        for i, field in enumerate(fields):
            at = 0
            for j, (first, width) in enumerate(spans):
                source = field.at[:, rows, pl.ds(first, width)]
                target = held.at[i, :, rows, pl.ds(at, width)]
                out.append(pltpu.make_async_copy(source, target, arrived.at[i, step, j]))
                at += width
        return out

    for step in range(steps):
        for copy in copies(step):
            copy.start()
    for copy in before:
        copy.start()

    def body(step, _):
        for copy in copies(step):
            copy.wait()
        for half in range(CHUNK // 8):
            near = pl.ds(pl.multiple_of(step * CHUNK + half * 8, 8), 8)
            away = pl.ds(pl.multiple_of(ROWS - 8 - step * CHUNK - half * 8, 8), 8)
            totals = [jnp.zeros((8, PART), jnp.float32) for _ in range(3)]
            for level in range(LEV):
                layer = (0.5 + level / LEV) / LEV
                along = layer * held[0, level, near, :]
                across = layer * held[1, level, near, :]
                wind_e = held[2, level, near, :]
                wind_n = held[3, level, near, :]
                totals[0] = totals[0] + along
                totals[1] = totals[1] + (along * wind_e + across * wind_n)
                totals[2] = totals[2] + (along * wind_n - across * wind_e)
            for i, total in enumerate(totals):
                own[i, near, :] = total
                far[i, away, :] = reversed_rows(total)
        return 0

    lax.fori_loop(0, steps, body, 0)
    for copy in before:
        copy.wait()


def outer_kernel(
    pedersen, hall, east_wind, north_wind, ions,
    to_left, to_right, own, far, held, source, held_ions, arrived, ions_arrived,
):
    last = COLS - LANES
    spans = ((0, LANES), (last, LANES))
    copies = [
        pltpu.make_async_copy(
            ions.at[:, :, pl.ds(first, LANES)],
            held_ions.at[:, :, pl.ds(i * LANES, LANES)],
            ions_arrived.at[i],
        )
        for i, (first, _) in enumerate(spans)
    ]
    sum_levels((pedersen, hall, east_wind, north_wind), spans, held, arrived, own, far, copies)
    for v, (sums, lines) in enumerate(((own, held_ions), (far, None))):
        rows = pl.ds(v * LINES, LINES)
        write_strips(sums, lines, source, (to_left.at[rows], to_right.at[rows]))


def inner_kernel(pedersen, hall, east_wind, north_wind, own, far, held, arrived):
    spans = ((LANES, PART),)
    sum_levels((pedersen, hall, east_wind, north_wind), spans, held, arrived, own, far)


def level_sums(kernel, name, shapes, scratch, parts, *fields):
    sums = jax.ShapeDtypeStruct((3, ROWS, PART), jnp.float32)
    out = [jax.ShapeDtypeStruct(shape, jnp.float32) for shape in shapes] + [sums, sums]
    steps = ROWS // CHUNK
    return pl.pallas_call(
        kernel,
        in_specs=[pl.BlockSpec(memory_space=pltpu.HBM)] * len(fields),
        out_specs=[pl.BlockSpec(memory_space=pltpu.VMEM)] * len(out),
        out_shape=out,
        scratch_shapes=[pltpu.VMEM((4, LEV, ROWS, PART), jnp.float32)]
        + [pltpu.VMEM(shape, jnp.float32) for shape in scratch]
        + [pltpu.SemaphoreType.DMA((4, steps, parts))]
        + ([pltpu.SemaphoreType.DMA((2,))] if scratch else []),
        compiler_params=pltpu.CompilerParams(vmem_limit_bytes=COLUMN_BYTES),
        cost_estimate=pl.CostEstimate(flops=1 << 23, bytes_accessed=1 << 23, transcendentals=0),
        name=name,
    )(*fields)


def turned_back(strip):
    rest = jnp.zeros((LANES - LINES, LANES), jnp.float32)
    return jnp.concatenate([strip[...], rest], 0).T


def gather_columns(outer, inner, fields):
    for i, field in enumerate(fields):
        field[:, :LANES] = outer[i, :, :LANES]
        field[:, LANES : COLS - LANES] = inner[i]
        field[:, COLS - LANES :] = outer[i, :, LANES:]


def write_edges(fields, from_right, from_left, ions, source, edges, everything):
    sigma, east, north = fields
    last = COLS - LANES
    for start in range(0, ROWS, 8):
        outer = everything or start < EDGE or start >= ROWS - EDGE
        local_source(east, north, source, start, range(TILES) if outer else (0, TILES - 1))
    right, left = (turned_back(from_right), turned_back(from_left))
    blank = jnp.zeros((ROWS, LANES), jnp.float32)
    sigma_x = put_lanes(blank, right, 0, 0, EDGE)
    sigma_x = put_lanes(sigma_x, right, SIGMA_PLUS, EDGE, 1)
    sigma_x = put_lanes(sigma_x, left, 0, LANES - EDGE, EDGE)
    sigma_x = put_lanes(sigma_x, left, SIGMA_PLUS, LANES - EDGE - 1, 1)
    source_x = put_lanes(blank, right, EDGE, 0, EDGE)
    source_x = put_lanes(source_x, left, EDGE, LANES - EDGE, EDGE)
    source_x = source_x - 0.5 * put_lanes(blank, east[:, last:], LANES - 1, 0, 1)
    source_x = source_x + 0.5 * put_lanes(blank, east[:, :LANES], 0, LANES - 1, 1)
    source[:, :LANES] += put_lanes(blank, -0.5 * left, CURRENT, 0, 1)
    source[:, last:] += put_lanes(blank, 0.5 * right, CURRENT, LANES - 1, 1)

    lane = lane_index(1)
    row = row_index(8)
    wide = row_index(8, COLS)
    for side in range(2):
        first = side * (ROWS - EDGE)
        rows = slice(first, first + EDGE)
        edges[side, :EDGE, :COLS] = sigma[rows]
        edges[side, EDGE:SIGMA_PLUS, :COLS] = source[rows]
        edges[side, :EDGE, COLS:WIDE] = sigma_x[rows]
        edges[side, EDGE:SIGMA_PLUS, COLS:WIDE] = source_x[rows]
        if side == 0:
            further, line = (sigma[EDGE : EDGE + 8][:1], north[0:8][:1])
            further_x = sigma_x[EDGE : EDGE + 1]
        else:
            further, line = (sigma[first - 8 : first][7:8], north[ROWS - 8 :][7:8])
            further_x = sigma_x[first - 1 : first]
        tile = jnp.where(wide == 0, further, 0.0)
        tile = jnp.where(wide == CURRENT - SIGMA_PLUS, line, tile)
        if ions is not None:
            for s in range(3):
                line = ions[s, ROWS - 8 :][7:8] if side else ions[s, :8][:1]
                tile = jnp.where(wide == IONS - SIGMA_PLUS + s, line, tile)
        edges[side, SIGMA_PLUS:, :COLS] = tile
        line = NORTH - SIGMA_PLUS + side
        north_x = jnp.where(
            lane < LANES // 2, from_right[SIGMA_PLUS:][line:][:1], from_left[SIGMA_PLUS:][line:][:1]
        )
        tile = jnp.where(row == 0, further_x, 0.0)
        edges[side, SIGMA_PLUS:, COLS:WIDE] = jnp.where(row == CURRENT - SIGMA_PLUS, north_x, tile)
        strip = put_lanes(blank, sigma_x, side * (LANES - EDGE - 1), 0, EDGE + 1)
        strip = put_lanes(strip, source_x, side * (LANES - EDGE), EDGE + 1, EDGE)
        edges[side, :, WIDE:] = strip.T[:LINES]


def far_kernel(outer, inner, from_right, from_left, edges, sigma, east, north, source):
    fields = (sigma, east, north)
    gather_columns(outer, inner, fields)
    rows = pl.ds(LINES, LINES)
    write_edges(fields, from_right.at[rows], from_left.at[rows], None, source, edges, False)


def piece_kernel(
    outer_far, inner_far, outer, inner, from_right, from_left, ions,
    middle, own_edges, own_middle, sigma, east, north, source, spare,
):
    fields = (sigma, east, north)
    for v, sums, out in ((1, (outer_far, inner_far), middle), (0, (outer, inner), own_middle)):
        gather_columns(*sums, fields)
        rows = pl.ds(v * LINES, LINES)
        write_edges(
            fields, from_right.at[rows], from_left.at[rows], None if v else ions, source,
            spare if v else own_edges, True,
        )
        out[0] = sigma[EDGE : ROWS - EDGE]
        out[1] = source[EDGE : ROWS - EDGE]


def build(kernel, name, shapes, spare, *fields):
    whole = pl.BlockSpec(memory_space=pltpu.VMEM)
    return pl.pallas_call(
        kernel,
        in_specs=[whole] * len(fields),
        out_specs=[whole] * len(shapes),
        out_shape=[jax.ShapeDtypeStruct(shape, jnp.float32) for shape in shapes],
        scratch_shapes=[pltpu.VMEM((ROWS, COLS), jnp.float32)] * 4
        + [pltpu.VMEM(shape, jnp.float32) for shape in spare],
        compiler_params=pltpu.CompilerParams(vmem_limit_bytes=VMEM_BYTES),
        name=name,
    )(*fields)


def band_kernel(band, own, far, to_chip, to_next):
    odd = lax.rem(band[0], 2)
    to_chip[...] = own[1 - odd, :, :WIDE] + far[1 - odd, :, :WIDE]
    to_next[...] = own[odd, :, :WIDE] + far[odd, :, :WIDE]


def bands_to_send(band, *fields):
    shape = jax.ShapeDtypeStruct((LINES, WIDE), jnp.float32)
    whole = pl.BlockSpec(memory_space=pltpu.VMEM)
    return pl.pallas_call(
        band_kernel,
        in_specs=[pl.BlockSpec(memory_space=pltpu.SMEM)] + [whole] * len(fields),
        out_specs=[whole] * 2,
        out_shape=[shape, shape],
        compiler_params=pltpu.CompilerParams(vmem_limit_bytes=VMEM_BYTES),
        name="lat_bands",
    )(band, *fields)


def solve_kernel(
    factors, band, own_edges, far_edges, from_chip, from_next, own_middle, far_middle,
    potential, drift_east, drift_north, fastest,
    sigma, sigma_next, sigma_prev, half_inverse, scaled_source, update, field_a, field_b, carried_a, carried_b,
    ours, theirs,
):
    theta = 0.5 * (HIGH_BOUND + LOW_BOUND)
    fields = (field_a, field_b)
    fluxes = (carried_a, carried_b)
    odd = lax.rem(band[0], 2)
    ours[...] = own_edges[:, :, :WIDE] + far_edges[:, :, :WIDE]
    theirs[1 - odd] = from_chip[...]
    theirs[odd] = from_next[...]
    top, bottom = (ours.at[0], ours.at[1])
    above, below = (theirs.at[0], theirs.at[1])
    count = TILES + 1
    spans = [slice(t * LANES, (t + 1) * LANES) for t in range(count)]
    middle = slice(EDGE, ROWS - EDGE)
    row = row_index(8)
    low = HALO + ROWS

    blank = jnp.zeros((ROWS, LANES), jnp.float32)
    right = turned_back(own_edges[0, :, WIDE:] + far_edges[0, :, WIDE:])
    left = turned_back(own_edges[1, :, WIDE:] + far_edges[1, :, WIDE:])
    sigma_x = put_lanes(blank, right, 0, 0, EDGE + 1)
    sigma_x = put_lanes(sigma_x, left, 0, LANES - EDGE - 1, EDGE + 1)
    source_x = put_lanes(blank, right, EDGE + 1, 0, EDGE)
    source_x = put_lanes(source_x, left, EDGE + 1, LANES - EDGE, EDGE)

    for t in range(count):
        span = spans[t]
        for piece, at in ((above, HALO - EDGE), (top, HALO), (bottom, low - EDGE), (below, low)):
            sigma[t, at : at + EDGE] = piece[:EDGE, span]
            scaled_source[t, at : at + EDGE] = piece[EDGE : 2 * EDGE, span]
        outer = above[SIGMA_PLUS:, span][:1]
        sigma[t, :8] = jnp.where(row == 7, outer, 0.0)
        outer = below[SIGMA_PLUS:, span][:1]
        sigma[t, EXT - 8 :] = jnp.where(row == 0, outer, 0.0)
        inner = slice(HALO + EDGE, low - EDGE)
        if t < TILES:
            sigma[t, inner] = own_middle[0, :, span] + far_middle[0, :, span]
            source = own_middle[1, :, span] + far_middle[1, :, span]
        else:
            sigma[t, inner] = sigma_x[middle]
            source = source_x[middle]
        scaled_source[t, inner] = source
        for at, spot, piece, half in (
            (HALO - 8, 7, top, 0.5),
            (HALO, 0, above, -0.5),
            (low - 8, 7, below, 0.5),
            (low, 0, bottom, -0.5),
        ):
            line = half * piece[SIGMA_PLUS:, span][CURRENT - SIGMA_PLUS :][:1]
            tile = scaled_source[t, at : at + 8]
            scaled_source[t, at : at + 8] = tile + jnp.where(row == spot, line, 0.0)

    first_band = band[0] == 0
    last_band = band[0] == band[1] - 1
    blank = jnp.zeros((8, LANES), jnp.float32)
    for t in range(count):
        for slot in range(2):
            for at in (0, EXT - 8):
                fields[slot][t, at : at + 8] = blank
                fluxes[slot][t, at : at + 8] = blank

    for start in range(8, EXT - 8, 8):
        here = [sigma[t, start : start + 8] for t in range(count)]
        sides = [sigma[t, start - 1 : start + 7] + sigma[t, start + 1 : start + 9] for t in range(count)]
        tall = [here[t] + 0.5 * sides[t] for t in range(count)]
        left = shifted(tall, True)
        right = shifted(tall, False)
        following = shifted(here, False)
        preceding = shifted(here, True)
        outside = None
        if start < HALO:
            outside = first_band
        if start >= HALO + ROWS:
            outside = last_band
        for t in range(count):
            diagonal = 0.5 * (6.0 * here[t] + (sides[t] + (left[t] + right[t]))) + DAMPING
            inverse = 1.0 / diagonal
            if outside is not None:
                inverse = jnp.where(outside, 0.0, inverse)
            source = scaled_source[t, start : start + 8] * inverse
            initial = source * (1.0 / theta)
            sigma_next[t, start : start + 8] = following[t]
            sigma_prev[t, start : start + 8] = preceding[t]
            half_inverse[t, start : start + 8] = 0.5 * inverse
            scaled_source[t, start : start + 8] = source
            update[t, start : start + 8] = initial
            field_b[t, start : start + 8] = initial
            carried_b[t, start : start + 8] = here[t] * initial

    def sweep(k, now, later, low, high):
        field_now, carried_now = (fields[now], fluxes[now])
        field_later, carried_later = (fields[later], fluxes[later])
        keep = factors[0, k - 1]
        gain = factors[1, k - 1]
        for start in range(low, high, 8):
            rows = slice(start, start + 8)
            upper = slice(start - 1, start + 7)
            lower = slice(start + 1, start + 9)
            centre, eastward, westward = ([], [], [])
            for t in range(count):
                value = field_now[t, rows]
                flux = carried_now[t, rows]
                value_sides = field_now[t, upper] + field_now[t, lower]
                flux_sides = carried_now[t, upper] + carried_now[t, lower]
                tall = value + 0.5 * value_sides
                flux_tall = flux + 0.5 * flux_sides
                centre.append(sigma[t, rows] * value_sides + flux_sides)
                eastward.append(sigma_next[t, rows] * tall + flux_tall)
                westward.append(sigma_prev[t, rows] * tall + flux_tall)
            from_west = shifted(eastward, True)
            from_east = shifted(westward, False)
            for t in range(count):
                total = centre[t] + (from_west[t] + from_east[t])
                value = field_now[t, rows]
                residual = (scaled_source[t, rows] - value) + half_inverse[t, rows] * total
                step = keep * update[t, rows] + gain * residual
                update[t, rows] = step
                value = value + step
                field_later[t, rows] = value
                carried_later[t, rows] = sigma[t, rows] * value

    def early(pair, _):
        sweep(2 * pair + 1, 1, 0, 8, EXT - 8)
        sweep(2 * pair + 2, 0, 1, 8, EXT - 8)
        return 0

    def late(pair, _):
        sweep(2 * pair + 9, 1, 0, 16, EXT - 16)
        sweep(2 * pair + 10, 0, 1, 16, EXT - 16)
        return 0

    lax.fori_loop(0, 4, early, 0)
    lax.fori_loop(0, 3, late, 0)
    sweep(15, 1, 0, 16, EXT - 16)

    last = fields[SWEEPS % 2]
    top_speed = jnp.zeros((8, LANES), jnp.float32)
    for start in range(HALO, HALO + ROWS, 8):
        rows = slice(start, start + 8)
        out = slice(start - HALO, start - HALO + 8)
        tiles = [last[t, rows] for t in range(count)]
        west = shifted(tiles, True)
        east = shifted(tiles, False)
        for t in range(TILES):
            potential[out, spans[t]] = tiles[t]
            lift = -0.5 * (last[t, start + 1 : start + 9] - last[t, start - 1 : start + 7])
            shove = 0.5 * (east[t] - west[t])
            drift_east[out, spans[t]] = lift
            drift_north[out, spans[t]] = shove
            top_speed = jnp.maximum(top_speed, jnp.abs(lift) + jnp.abs(shove))
    peak = jnp.max(top_speed, axis=1, keepdims=True)
    peak = jnp.max(peak, axis=0, keepdims=True)
    fastest[...] = jnp.broadcast_to(peak[None], fastest.shape)


def solve(peers, factors, band, *fields):
    shapes = [(ROWS, COLS)] * 3 + [(peers, 1, LANES)]
    plane = (TILES + 1, EXT, LANES)
    memory = pltpu.VMEM(plane, jnp.float32)
    return pl.pallas_call(
        solve_kernel,
        in_specs=[pl.BlockSpec(memory_space=pltpu.SMEM)] * 2
        + [pl.BlockSpec(memory_space=pltpu.VMEM)] * len(fields),
        out_specs=[pl.BlockSpec(memory_space=pltpu.VMEM)] * 4,
        out_shape=[jax.ShapeDtypeStruct(shape, jnp.float32) for shape in shapes],
        scratch_shapes=[memory] * 10 + [pltpu.VMEM((2, LINES, WIDE), jnp.float32)] * 2,
        compiler_params=pltpu.CompilerParams(vmem_limit_bytes=VMEM_BYTES),
        name="potential_solve",
    )(factors, band, *fields)


def advect_kernel(
    band, fastest, drift_east, drift_north, ions, from_chip, from_next, from_right, from_left, out, theirs
):
    odd = lax.rem(band[0], 2)
    theirs[1 - odd] = from_chip[SIGMA_PLUS:]
    theirs[odd] = from_next[SIGMA_PLUS:]
    above, below = (theirs.at[0], theirs.at[1])
    peak = jnp.max(fastest[...], axis=0)
    peak = jnp.max(peak, axis=1, keepdims=True)
    time_step = COURANT / (peak + 1e-06)
    lane = lane_index(ROWS)
    wide = row_index(ROWS, LANES)
    beyond_right, beyond_left = (turned_back(from_right[:LINES]), turned_back(from_left[:LINES]))
    for s in range(3):
        pace = MOBILITY[s] * time_step
        tiles = [ions[s, :, t * LANES : (t + 1) * LANES] for t in range(TILES)]
        left = [pltpu.roll(tile, 1, 1) for tile in tiles]
        right = [pltpu.roll(tile, LANES - 1, 1) for tile in tiles]
        edge_right = pltpu.roll(beyond_right, LANES - 1 - IONS - s, 1)
        edge_left = pltpu.roll(beyond_left, LANES - IONS - s, 1)
        for t in range(TILES):
            span = slice(t * LANES, (t + 1) * LANES)
            density = tiles[t]
            west = jnp.where(lane == 0, left[t - 1] if t else edge_left, left[t])
            east = jnp.where(lane == LANES - 1, right[t + 1] if t < TILES - 1 else edge_right, right[t])
            behind = above[:, span][IONS - SIGMA_PLUS + s :][:1]
            ahead = below[:, span][IONS - SIGMA_PLUS + s :][:1]
            south = jnp.where(wide == 0, behind, pltpu.roll(density, 1, 0))
            north = jnp.where(wide == ROWS - 1, ahead, pltpu.roll(density, ROWS - 1, 0))
            cross_east = pace * drift_east[:, span]
            cross_north = pace * drift_north[:, span]
            result = density - jnp.maximum(cross_east, 0.0) * (density - west)
            result = result - jnp.minimum(cross_east, 0.0) * (east - density)
            result = result - jnp.maximum(cross_north, 0.0) * (density - south)
            result = result - jnp.minimum(cross_north, 0.0) * (north - density)
            out[s, :, span] = result


def advect(band, *fields):
    whole = pl.BlockSpec(memory_space=pltpu.VMEM)
    return pl.pallas_call(
        advect_kernel,
        in_specs=[pl.BlockSpec(memory_space=pltpu.SMEM)] + [whole] * len(fields),
        out_specs=whole,
        out_shape=jax.ShapeDtypeStruct((3, ROWS, COLS), jnp.float32),
        scratch_shapes=[pltpu.VMEM((2, 8, WIDE), jnp.float32)],
        compiler_params=pltpu.CompilerParams(vmem_limit_bytes=VMEM_BYTES),
        name="ion_advection",
    )(band, *fields)


def shards(pedersen, hall_conductivity, east_wind, north_wind, ion_density):
    lats = lax.axis_size("lat")
    lons = lax.axis_size("lon")
    mirror = [(i, lats - 1 - i) for i in range(lats)]
    eastward = [(i, (i + 1) % lons) for i in range(lons)]
    westward = [(j, i) for i, j in eastward]
    chip = [(i, i ^ 1) for i in range(lats)]
    beyond = [(i, i + 1 if i % 2 else i - 1) for i in range(1, lats - 1)]
    band = jnp.stack([lax.axis_index("lat").astype(jnp.int32), jnp.int32(lats)])

    levels = (pedersen, hall_conductivity, east_wind, north_wind)
    strip = (2 * LINES, LANES)
    to_left, to_right, outer, outer_far = level_sums(
        outer_kernel, "outer_sums", [strip] * 2, [(ROWS, PART), (3, ROWS, PART)], 2, *levels, ion_density
    )
    from_right = lax.ppermute(to_left, "lon", westward)
    from_left = lax.ppermute(to_right, "lon", eastward)
    inner, inner_far = level_sums(inner_kernel, "inner_sums", [], [], 1, *levels)
    (edges,) = build(
        far_kernel, "wide_edges", [(2, LINES, SEND)], [], outer_far, inner_far, from_right, from_left
    )
    far_edges = lax.ppermute(edges, "lat", mirror)
    middle, own_edges, own_middle = build(
        piece_kernel, "pieces", [(2, MID, COLS), (2, LINES, SEND), (2, MID, COLS)], [(2, LINES, SEND)],
        outer_far, inner_far, outer, inner, from_right, from_left, ion_density,
    )
    far_middle = lax.ppermute(middle, "lat", mirror)
    to_chip, to_next = bands_to_send(band, own_edges, far_edges)
    from_chip = lax.ppermute(to_chip, "lat", chip)
    from_next = lax.ppermute(to_next, "lat", beyond)

    theta, first_list, second_list = chebyshev_factors()
    factors = jnp.array([first_list, second_list], jnp.float32)
    potential, drift_east, drift_north, peaks = solve(
        lats * lons, factors, band, own_edges, far_edges, from_chip, from_next, own_middle, far_middle
    )
    peaks = lax.all_to_all(peaks, ("lat", "lon"), 0, 0, tiled=True)
    ion_update = advect(
        band, peaks, drift_east, drift_north, ion_density, from_chip, from_next, from_right, from_left
    )
    return (potential, ion_update)


def solution(mesh):
    spec = P(None, "lat", "lon")
    return jax.shard_map(
        shards,
        mesh=mesh,
        in_specs=(spec,) * 5,
        out_specs=(P("lat", "lon"), spec),
        check_vma=False,
    )
```

```python
import functools

import jax
import jax.numpy as jnp
from jax import lax
from jax.experimental import pallas as pl
from jax.experimental.pallas import tpu as pltpu
from jax.sharding import PartitionSpec as P

LEV = 16
SWEEPS = 16
DAMPING = 0.0001
LOW_BOUND = 0.05
HIGH_BOUND = 2.0
COURANT = 0.8
MOBILITY = (1.0, 0.6, 0.3)

LANES = 128
ROWS = 128
COLS = 512
TILES = COLS // LANES
WIDE = COLS + LANES
SEND = WIDE + LANES
PART = COLS // 2
EDGE = 16
HALO = 24
MID = ROWS - 2 * EDGE
EXT = ROWS + 2 * HALO
SIGMA_PLUS = 2 * EDGE
CURRENT = SIGMA_PLUS + 1
IONS = SIGMA_PLUS + 2
NORTH = SIGMA_PLUS + 5
LINES = SIGMA_PLUS + 8
CHUNK = 16
VMEM_BYTES = 32 * 1024 * 1024
COLUMN_BYTES = 51 * 1024 * 1024


def chebyshev_factors():
    theta = 0.5 * (HIGH_BOUND + LOW_BOUND)
    delta = 0.5 * (HIGH_BOUND - LOW_BOUND)
    sigma_one = theta / delta
    rho_prev = 1.0 / sigma_one
    first_list = []
    second_list = []
    for sweep in range(SWEEPS):
        rho_next = 1.0 / (2.0 * sigma_one - rho_prev)
        first_list.append(rho_next * rho_prev)
        second_list.append(2.0 * rho_next / delta)
        rho_prev = rho_next
    return (theta, first_list, second_list)


def lane_index(rows):
    return lax.broadcasted_iota(jnp.int32, (rows, LANES), 1)


def row_index(rows, cols=LANES):
    return lax.broadcasted_iota(jnp.int32, (rows, cols), 0)


def reversed_rows(tile):
    row = row_index(8, tile.shape[1])
    tile = pltpu.roll(tile, 4, 0)
    tile = jnp.where((row & 2) == 0, pltpu.roll(tile, 6, 0), pltpu.roll(tile, 2, 0))
    return jnp.where((row & 1) == 0, pltpu.roll(tile, 7, 0), pltpu.roll(tile, 1, 0))


def shifted(tiles, to_right):
    count = len(tiles)
    lane = lane_index(tiles[0].shape[0])
    if to_right:
        turned = [pltpu.roll(tile, 1, 1) for tile in tiles]
        return [jnp.where(lane == 0, turned[t - 1], turned[t]) for t in range(count)]
    turned = [pltpu.roll(tile, LANES - 1, 1) for tile in tiles]
    return [jnp.where(lane == LANES - 1, turned[(t + 1) % count], turned[t]) for t in range(count)]


def local_source(east, north, source, start, wanted):
    rows = slice(start, start + 8)
    lane = lane_index(8)
    row = row_index(8)
    zero = jnp.zeros((8, LANES), jnp.float32)
    tiles = east.shape[1] // LANES
    for t in wanted:
        span = slice(t * LANES, (t + 1) * LANES)
        tile = east[rows, span]
        left = right = zero
        if t:
            left = pltpu.roll(east[rows, (t - 1) * LANES : t * LANES], 1, 1)
        if t < tiles - 1:
            right = pltpu.roll(east[rows, (t + 1) * LANES : (t + 2) * LANES], LANES - 1, 1)
        before = jnp.where(lane == 0, left, pltpu.roll(tile, 1, 1))
        after = jnp.where(lane == LANES - 1, right, pltpu.roll(tile, LANES - 1, 1))
        here = north[rows, span]
        above = north[start - 8 : start, span][7:8] if start else zero[:1]
        below = north[start + 8 : start + 16, span][:1] if start + 8 < ROWS else zero[:1]
        up = jnp.where(row == 0, above, pltpu.roll(here, 1, 0))
        down = jnp.where(row == 7, below, pltpu.roll(here, 7, 0))
        source[rows, span] = 0.5 * (after - before) + 0.5 * (down - up)


def put_lanes(tile, source, at, first, count):
    lane = lane_index(tile.shape[0])
    turn = (first - at) % LANES
    moved = pltpu.roll(source, turn, 1) if turn else source
    return jnp.where((lane >= first) & (lane < first + count), moved, tile)


def write_strips(sums, source, strips):
    sigma, east, north = (sums.at[0], sums.at[1], sums.at[2])
    for start in range(0, ROWS, 8):
        local_source(east, north, source, start, (0, 1))
    row = row_index(8)
    for side, out in enumerate(strips):
        span = slice(side * LANES, (side + 1) * LANES)
        near = side * (LANES - EDGE)
        strip = jnp.zeros((ROWS, LANES), jnp.float32)
        strip = put_lanes(strip, sigma[:, span], near, 0, EDGE)
        strip = put_lanes(strip, source[:, span], near, EDGE, EDGE)
        strip = put_lanes(strip, sigma[:, span], LANES - EDGE - 1 if side else EDGE, SIGMA_PLUS, 1)
        strip = put_lanes(strip, east[:, span], side * (LANES - 1), CURRENT, 1)
        turned = strip.T
        out[:SIGMA_PLUS] = turned[:SIGMA_PLUS]
        tile = turned[SIGMA_PLUS:LINES]
        tile = jnp.where(row == NORTH - SIGMA_PLUS, north[0:8, span][:1], tile)
        out[SIGMA_PLUS:] = jnp.where(row == NORTH + 1 - SIGMA_PLUS, north[ROWS - 8 :, span][7:8], tile)


def sum_levels(fields, spans, held, arrived, own, far):
    steps = ROWS // CHUNK

    def copies(step):
        rows = pl.ds(pl.multiple_of(step * CHUNK, CHUNK), CHUNK)
        out = []
        for i, field in enumerate(fields):
            at = 0
            for j, (first, width) in enumerate(spans):
                source = field.at[:, rows, pl.ds(first, width)]
                target = held.at[i, :, rows, pl.ds(at, width)]
                out.append(pltpu.make_async_copy(source, target, arrived.at[i, step, j]))
                at += width
        return out

    for step in range(steps):
        for copy in copies(step):
            copy.start()

    def body(step, _):
        for copy in copies(step):
            copy.wait()
        for half in range(CHUNK // 8):
            near = pl.ds(pl.multiple_of(step * CHUNK + half * 8, 8), 8)
            away = pl.ds(pl.multiple_of(ROWS - 8 - step * CHUNK - half * 8, 8), 8)
            totals = [jnp.zeros((8, PART), jnp.float32) for _ in range(3)]
            for level in range(LEV):
                layer = (0.5 + level / LEV) / LEV
                along = layer * held[0, level, near, :]
                across = layer * held[1, level, near, :]
                wind_e = held[2, level, near, :]
                wind_n = held[3, level, near, :]
                totals[0] = totals[0] + along
                totals[1] = totals[1] + (along * wind_e + across * wind_n)
                totals[2] = totals[2] + (along * wind_n - across * wind_e)
            for i, total in enumerate(totals):
                own[i, near, :] = total
                far[i, away, :] = reversed_rows(total)
        return 0

    lax.fori_loop(0, steps, body, 0)


def outer_kernel(
    pedersen, hall, east_wind, north_wind, to_left, to_right, own, far, held, arrived, source
):
    spans = ((0, LANES), (COLS - LANES, LANES))
    sum_levels((pedersen, hall, east_wind, north_wind), spans, held, arrived, own, far)
    for v, sums in enumerate((own, far)):
        rows = pl.ds(v * LINES, LINES)
        write_strips(sums, source, (to_left.at[rows], to_right.at[rows]))


def ion_kernel(left, right, ions, to_left, to_right):
    row = row_index(8)
    for side, strip, out in ((0, left, to_left), (1, right, to_right)):
        at = side * (COLS - LANES)
        tile = strip[SIGMA_PLUS:LINES]
        for s in range(3):
            turned = ions[s, :, at : at + LANES].T
            line = turned[LANES - 1 :] if side else turned[:1]
            tile = jnp.where(row == IONS - SIGMA_PLUS + s, line, tile)
        out[...] = strip[...]
        out[SIGMA_PLUS:LINES] = tile


def inner_kernel(pedersen, hall, east_wind, north_wind, own, far, held, arrived):
    spans = ((LANES, PART),)
    sum_levels((pedersen, hall, east_wind, north_wind), spans, held, arrived, own, far)


def level_sums(kernel, name, shapes, scratch, parts, *fields):
    sums = jax.ShapeDtypeStruct((3, ROWS, PART), jnp.float32)
    out = [jax.ShapeDtypeStruct(shape, jnp.float32) for shape in shapes] + [sums, sums]
    steps = ROWS // CHUNK
    return pl.pallas_call(
        kernel,
        in_specs=[pl.BlockSpec(memory_space=pltpu.HBM)] * len(fields),
        out_specs=[pl.BlockSpec(memory_space=pltpu.VMEM)] * len(out),
        out_shape=out,
        scratch_shapes=[pltpu.VMEM((4, LEV, ROWS, PART), jnp.float32)]
        + [pltpu.SemaphoreType.DMA((4, steps, parts))]
        + [pltpu.VMEM(shape, jnp.float32) for shape in scratch],
        compiler_params=pltpu.CompilerParams(vmem_limit_bytes=COLUMN_BYTES),
        cost_estimate=pl.CostEstimate(flops=1 << 23, bytes_accessed=1 << 23, transcendentals=0),
        name=name,
    )(*fields)


def turned_back(strip):
    rest = jnp.zeros((LANES - LINES, LANES), jnp.float32)
    return jnp.concatenate([strip[...], rest], 0).T


def gather_columns(outer, inner, fields):
    for i, field in enumerate(fields):
        field[:, :LANES] = outer[i, :, :LANES]
        field[:, LANES : COLS - LANES] = inner[i]
        field[:, COLS - LANES :] = outer[i, :, LANES:]


def write_edges(fields, from_right, from_left, ions, source, edges, everything):
    sigma, east, north = fields
    last = COLS - LANES
    for start in range(0, ROWS, 8):
        outer = everything or start < EDGE or start >= ROWS - EDGE
        local_source(east, north, source, start, range(TILES) if outer else (0, TILES - 1))
    right, left = (turned_back(from_right), turned_back(from_left))
    blank = jnp.zeros((ROWS, LANES), jnp.float32)
    sigma_x = put_lanes(blank, right, 0, 0, EDGE)
    sigma_x = put_lanes(sigma_x, right, SIGMA_PLUS, EDGE, 1)
    sigma_x = put_lanes(sigma_x, left, 0, LANES - EDGE, EDGE)
    sigma_x = put_lanes(sigma_x, left, SIGMA_PLUS, LANES - EDGE - 1, 1)
    source_x = put_lanes(blank, right, EDGE, 0, EDGE)
    source_x = put_lanes(source_x, left, EDGE, LANES - EDGE, EDGE)
    source_x = source_x - 0.5 * put_lanes(blank, east[:, last:], LANES - 1, 0, 1)
    source_x = source_x + 0.5 * put_lanes(blank, east[:, :LANES], 0, LANES - 1, 1)
    source[:, :LANES] += put_lanes(blank, -0.5 * left, CURRENT, 0, 1)
    source[:, last:] += put_lanes(blank, 0.5 * right, CURRENT, LANES - 1, 1)

    lane = lane_index(1)
    row = row_index(8)
    wide = row_index(8, COLS)
    for side in range(2):
        first = side * (ROWS - EDGE)
        rows = slice(first, first + EDGE)
        edges[side, :EDGE, :COLS] = sigma[rows]
        edges[side, EDGE:SIGMA_PLUS, :COLS] = source[rows]
        edges[side, :EDGE, COLS:WIDE] = sigma_x[rows]
        edges[side, EDGE:SIGMA_PLUS, COLS:WIDE] = source_x[rows]
        if side == 0:
            further, line = (sigma[EDGE : EDGE + 8][:1], north[0:8][:1])
            further_x = sigma_x[EDGE : EDGE + 1]
        else:
            further, line = (sigma[first - 8 : first][7:8], north[ROWS - 8 :][7:8])
            further_x = sigma_x[first - 1 : first]
        tile = jnp.where(wide == 0, further, 0.0)
        tile = jnp.where(wide == CURRENT - SIGMA_PLUS, line, tile)
        if ions is not None:
            for s in range(3):
                line = ions[s, ROWS - 8 :][7:8] if side else ions[s, :8][:1]
                tile = jnp.where(wide == IONS - SIGMA_PLUS + s, line, tile)
        edges[side, SIGMA_PLUS:, :COLS] = tile
        line = NORTH - SIGMA_PLUS + side
        north_x = jnp.where(
            lane < LANES // 2, from_right[SIGMA_PLUS:][line:][:1], from_left[SIGMA_PLUS:][line:][:1]
        )
        tile = jnp.where(row == 0, further_x, 0.0)
        edges[side, SIGMA_PLUS:, COLS:WIDE] = jnp.where(row == CURRENT - SIGMA_PLUS, north_x, tile)
        strip = put_lanes(blank, sigma_x, side * (LANES - EDGE - 1), 0, EDGE + 1)
        strip = put_lanes(strip, source_x, side * (LANES - EDGE), EDGE + 1, EDGE)
        edges[side, :, WIDE:] = strip.T[:LINES]


def far_kernel(outer, inner, from_right, from_left, edges, sigma, east, north, source):
    fields = (sigma, east, north)
    gather_columns(outer, inner, fields)
    rows = pl.ds(LINES, LINES)
    write_edges(fields, from_right.at[rows], from_left.at[rows], None, source, edges, False)


def piece_kernel(
    outer_far, inner_far, outer, inner, from_right, from_left, ions,
    far_sigma, far_source, own_edges, own_sigma, own_source, sigma, east, north, source, spare,
):
    fields = (sigma, east, north)
    for v, sums, out in (
        (1, (outer_far, inner_far), (far_sigma, far_source)),
        (0, (outer, inner), (own_sigma, own_source)),
    ):
        gather_columns(*sums, fields)
        rows = pl.ds(v * LINES, LINES)
        write_edges(
            fields, from_right.at[rows], from_left.at[rows], None if v else ions, source,
            spare if v else own_edges, True,
        )
        out[0][...] = sigma[EDGE : ROWS - EDGE]
        out[1][...] = source[EDGE : ROWS - EDGE]


def build(kernel, name, shapes, scratch, *fields):
    whole = pl.BlockSpec(memory_space=pltpu.VMEM)
    return pl.pallas_call(
        kernel,
        in_specs=[whole] * len(fields),
        out_specs=[whole] * len(shapes),
        out_shape=[jax.ShapeDtypeStruct(shape, jnp.float32) for shape in shapes],
        scratch_shapes=[pltpu.VMEM(shape, jnp.float32) for shape in scratch],
        compiler_params=pltpu.CompilerParams(vmem_limit_bytes=VMEM_BYTES),
        name=name,
    )(*fields)


def band_kernel(band, own, far, to_chip, to_next):
    odd = lax.rem(band[0], 2) == 1
    top, bottom = (own[side, :, :WIDE] + far[side, :, :WIDE] for side in range(2))
    to_chip[...] = jnp.where(odd, top, bottom)
    to_next[...] = jnp.where(odd, bottom, top)


def bands_to_send(band, *fields):
    shape = jax.ShapeDtypeStruct((LINES, WIDE), jnp.float32)
    whole = pl.BlockSpec(memory_space=pltpu.VMEM)
    return pl.pallas_call(
        band_kernel,
        in_specs=[pl.BlockSpec(memory_space=pltpu.SMEM)] + [whole] * len(fields),
        out_specs=[whole] * 2,
        out_shape=[shape, shape],
        compiler_params=pltpu.CompilerParams(vmem_limit_bytes=VMEM_BYTES),
        name="lat_bands",
    )(band, *fields)


def solve_kernel(
    factors, band, own_edges, far_edges, from_chip, from_next,
    own_sigma, own_source, far_sigma, far_source,
    potential, drift_east, drift_north, fastest,
    sigma, sigma_next, sigma_prev, half_inverse, scaled_source, update, field_a, field_b, carried_a, carried_b,
    ours, theirs,
):
    theta = 0.5 * (HIGH_BOUND + LOW_BOUND)
    fields = (field_a, field_b)
    fluxes = (carried_a, carried_b)
    odd = lax.rem(band[0], 2) == 1
    ours[...] = own_edges[:, :, :WIDE] + far_edges[:, :, :WIDE]
    theirs[0] = jnp.where(odd, from_chip[...], from_next[...])
    theirs[1] = jnp.where(odd, from_next[...], from_chip[...])
    top, bottom = (ours.at[0], ours.at[1])
    above, below = (theirs.at[0], theirs.at[1])
    count = TILES + 1
    spans = [slice(t * LANES, (t + 1) * LANES) for t in range(count)]
    middle = slice(EDGE, ROWS - EDGE)
    row = row_index(8)
    low = HALO + ROWS

    blank = jnp.zeros((ROWS, LANES), jnp.float32)
    right = turned_back(own_edges[0, :, WIDE:] + far_edges[0, :, WIDE:])
    left = turned_back(own_edges[1, :, WIDE:] + far_edges[1, :, WIDE:])
    sigma_x = put_lanes(blank, right, 0, 0, EDGE + 1)
    sigma_x = put_lanes(sigma_x, left, 0, LANES - EDGE - 1, EDGE + 1)
    source_x = put_lanes(blank, right, EDGE + 1, 0, EDGE)
    source_x = put_lanes(source_x, left, EDGE + 1, LANES - EDGE, EDGE)

    for t in range(count):
        span = spans[t]
        for piece, at in ((above, HALO - EDGE), (top, HALO), (bottom, low - EDGE), (below, low)):
            sigma[t, at : at + EDGE] = piece[:EDGE, span]
            scaled_source[t, at : at + EDGE] = piece[EDGE : 2 * EDGE, span]
        outer = above[SIGMA_PLUS:, span][:1]
        sigma[t, :8] = jnp.where(row == 7, outer, 0.0)
        outer = below[SIGMA_PLUS:, span][:1]
        sigma[t, EXT - 8 :] = jnp.where(row == 0, outer, 0.0)
        inner = slice(HALO + EDGE, low - EDGE)
        if t < TILES:
            sigma[t, inner] = own_sigma[:, span] + far_sigma[:, span]
            source = own_source[:, span] + far_source[:, span]
        else:
            sigma[t, inner] = sigma_x[middle]
            source = source_x[middle]
        scaled_source[t, inner] = source
        for at, spot, piece, half in (
            (HALO - 8, 7, top, 0.5),
            (HALO, 0, above, -0.5),
            (low - 8, 7, below, 0.5),
            (low, 0, bottom, -0.5),
        ):
            line = half * piece[SIGMA_PLUS:, span][CURRENT - SIGMA_PLUS :][:1]
            tile = scaled_source[t, at : at + 8]
            scaled_source[t, at : at + 8] = tile + jnp.where(row == spot, line, 0.0)

    first_band = band[0] == 0
    last_band = band[0] == band[1] - 1
    blank = jnp.zeros((8, LANES), jnp.float32)
    for t in range(count):
        for slot in range(2):
            for at in (0, EXT - 8):
                fields[slot][t, at : at + 8] = blank
                fluxes[slot][t, at : at + 8] = blank

    for start in range(8, EXT - 8, 8):
        here = [sigma[t, start : start + 8] for t in range(count)]
        sides = [sigma[t, start - 1 : start + 7] + sigma[t, start + 1 : start + 9] for t in range(count)]
        tall = [here[t] + 0.5 * sides[t] for t in range(count)]
        left = shifted(tall, True)
        right = shifted(tall, False)
        following = shifted(here, False)
        preceding = shifted(here, True)
        outside = None
        if start < HALO:
            outside = first_band
        if start >= HALO + ROWS:
            outside = last_band
        for t in range(count):
            diagonal = 0.5 * (6.0 * here[t] + (sides[t] + (left[t] + right[t]))) + DAMPING
            inverse = 1.0 / diagonal
            if outside is not None:
                inverse = jnp.where(outside, 0.0, inverse)
            source = scaled_source[t, start : start + 8] * inverse
            initial = source * (1.0 / theta)
            sigma_next[t, start : start + 8] = following[t]
            sigma_prev[t, start : start + 8] = preceding[t]
            half_inverse[t, start : start + 8] = 0.5 * inverse
            scaled_source[t, start : start + 8] = source
            update[t, start : start + 8] = initial
            field_b[t, start : start + 8] = initial
            carried_b[t, start : start + 8] = here[t] * initial

    def sweep(k, now, later, low, high):
        field_now, carried_now = (fields[now], fluxes[now])
        field_later, carried_later = (fields[later], fluxes[later])
        keep = factors[0, k - 1]
        gain = factors[1, k - 1]
        for start in range(low, high, 8):
            rows = slice(start, start + 8)
            upper = slice(start - 1, start + 7)
            lower = slice(start + 1, start + 9)
            centre, eastward, westward = ([], [], [])
            for t in range(count):
                value = field_now[t, rows]
                flux = carried_now[t, rows]
                value_sides = field_now[t, upper] + field_now[t, lower]
                flux_sides = carried_now[t, upper] + carried_now[t, lower]
                tall = value + 0.5 * value_sides
                flux_tall = flux + 0.5 * flux_sides
                centre.append(sigma[t, rows] * value_sides + flux_sides)
                eastward.append(sigma_next[t, rows] * tall + flux_tall)
                westward.append(sigma_prev[t, rows] * tall + flux_tall)
            from_west = shifted(eastward, True)
            from_east = shifted(westward, False)
            for t in range(count):
                total = centre[t] + (from_west[t] + from_east[t])
                value = field_now[t, rows]
                residual = (scaled_source[t, rows] - value) + half_inverse[t, rows] * total
                step = keep * update[t, rows] + gain * residual
                update[t, rows] = step
                value = value + step
                field_later[t, rows] = value
                carried_later[t, rows] = sigma[t, rows] * value

    def early(pair, _):
        sweep(2 * pair + 1, 1, 0, 8, EXT - 8)
        sweep(2 * pair + 2, 0, 1, 8, EXT - 8)
        return 0

    def late(pair, _):
        sweep(2 * pair + 9, 1, 0, 16, EXT - 16)
        sweep(2 * pair + 10, 0, 1, 16, EXT - 16)
        return 0

    lax.fori_loop(0, 4, early, 0)
    lax.fori_loop(0, 3, late, 0)
    sweep(15, 1, 0, 16, EXT - 16)

    last = fields[SWEEPS % 2]
    top_speed = jnp.zeros((8, LANES), jnp.float32)
    for start in range(HALO, HALO + ROWS, 8):
        rows = slice(start, start + 8)
        out = slice(start - HALO, start - HALO + 8)
        tiles = [last[t, rows] for t in range(count)]
        west = shifted(tiles, True)
        east = shifted(tiles, False)
        for t in range(TILES):
            potential[out, spans[t]] = tiles[t]
            lift = -0.5 * (last[t, start + 1 : start + 9] - last[t, start - 1 : start + 7])
            shove = 0.5 * (east[t] - west[t])
            drift_east[out, spans[t]] = lift
            drift_north[out, spans[t]] = shove
            top_speed = jnp.maximum(top_speed, jnp.abs(lift) + jnp.abs(shove))
    peak = jnp.max(top_speed, axis=1, keepdims=True)
    peak = jnp.max(peak, axis=0, keepdims=True)
    fastest[...] = jnp.broadcast_to(peak[None], fastest.shape)


def solve(peers, factors, band, *fields):
    shapes = [(ROWS, COLS)] * 3 + [(peers, 1, LANES)]
    plane = (TILES + 1, EXT, LANES)
    memory = pltpu.VMEM(plane, jnp.float32)
    return pl.pallas_call(
        solve_kernel,
        in_specs=[pl.BlockSpec(memory_space=pltpu.SMEM)] * 2
        + [pl.BlockSpec(memory_space=pltpu.VMEM)] * len(fields),
        out_specs=[pl.BlockSpec(memory_space=pltpu.VMEM)] * 4,
        out_shape=[jax.ShapeDtypeStruct(shape, jnp.float32) for shape in shapes],
        scratch_shapes=[memory] * 10 + [pltpu.VMEM((2, LINES, WIDE), jnp.float32)] * 2,
        compiler_params=pltpu.CompilerParams(vmem_limit_bytes=VMEM_BYTES),
        name="potential_solve",
    )(factors, band, *fields)


def advect_kernel(
    band, fastest, drift_east, drift_north, ions, from_chip, from_next, from_right, from_left, out
):
    odd = lax.rem(band[0], 2) == 1
    above = jnp.where(odd, from_chip[SIGMA_PLUS:, :COLS], from_next[SIGMA_PLUS:, :COLS])
    below = jnp.where(odd, from_next[SIGMA_PLUS:, :COLS], from_chip[SIGMA_PLUS:, :COLS])
    peak = jnp.max(fastest[...], axis=0)
    peak = jnp.max(peak, axis=1, keepdims=True)
    time_step = COURANT / (peak + 1e-06)
    lane = lane_index(ROWS)
    wide = row_index(ROWS, LANES)
    beyond_right, beyond_left = (turned_back(from_right[:LINES]), turned_back(from_left[:LINES]))
    for s in range(3):
        pace = MOBILITY[s] * time_step
        tiles = [ions[s, :, t * LANES : (t + 1) * LANES] for t in range(TILES)]
        left = [pltpu.roll(tile, 1, 1) for tile in tiles]
        right = [pltpu.roll(tile, LANES - 1, 1) for tile in tiles]
        edge_right = pltpu.roll(beyond_right, LANES - 1 - IONS - s, 1)
        edge_left = pltpu.roll(beyond_left, LANES - IONS - s, 1)
        for t in range(TILES):
            span = slice(t * LANES, (t + 1) * LANES)
            density = tiles[t]
            west = jnp.where(lane == 0, left[t - 1] if t else edge_left, left[t])
            east = jnp.where(lane == LANES - 1, right[t + 1] if t < TILES - 1 else edge_right, right[t])
            behind = above[:, span][IONS - SIGMA_PLUS + s :][:1]
            ahead = below[:, span][IONS - SIGMA_PLUS + s :][:1]
            south = jnp.where(wide == 0, behind, pltpu.roll(density, 1, 0))
            north = jnp.where(wide == ROWS - 1, ahead, pltpu.roll(density, ROWS - 1, 0))
            cross_east = pace * drift_east[:, span]
            cross_north = pace * drift_north[:, span]
            result = density - jnp.maximum(cross_east, 0.0) * (density - west)
            result = result - jnp.minimum(cross_east, 0.0) * (east - density)
            result = result - jnp.maximum(cross_north, 0.0) * (density - south)
            result = result - jnp.minimum(cross_north, 0.0) * (north - density)
            out[s, :, span] = result


def advect(band, *fields):
    whole = pl.BlockSpec(memory_space=pltpu.VMEM)
    return pl.pallas_call(
        advect_kernel,
        in_specs=[pl.BlockSpec(memory_space=pltpu.SMEM)] + [whole] * len(fields),
        out_specs=whole,
        out_shape=jax.ShapeDtypeStruct((3, ROWS, COLS), jnp.float32),
        compiler_params=pltpu.CompilerParams(vmem_limit_bytes=VMEM_BYTES),
        name="ion_advection",
    )(band, *fields)


def shards(pedersen, hall_conductivity, east_wind, north_wind, ion_density):
    lats = lax.axis_size("lat")
    lons = lax.axis_size("lon")
    mirror = [(i, lats - 1 - i) for i in range(lats)]
    eastward = [(i, (i + 1) % lons) for i in range(lons)]
    westward = [(j, i) for i, j in eastward]
    chip = [(i, i ^ 1) for i in range(lats)]
    beyond = [(i, i + 1 if i % 2 else i - 1) for i in range(1, lats - 1)]
    band = jnp.stack([lax.axis_index("lat").astype(jnp.int32), jnp.int32(lats)])

    levels = (pedersen, hall_conductivity, east_wind, north_wind)
    strip = (2 * LINES, LANES)
    left, right, outer, outer_far = level_sums(
        outer_kernel, "outer_sums", [strip] * 2, [(ROWS, PART)], 2, *levels
    )
    to_left, to_right = build(ion_kernel, "lon_strips", [strip] * 2, [], left, right, ion_density)
    from_right = lax.ppermute(to_left, "lon", westward)
    from_left = lax.ppermute(to_right, "lon", eastward)
    inner, inner_far = level_sums(inner_kernel, "inner_sums", [], [], 1, *levels)
    planes = [(ROWS, COLS)] * 4
    (edges,) = build(
        far_kernel, "wide_edges", [(2, LINES, SEND)], planes, outer_far, inner_far, from_right, from_left
    )
    far_edges = lax.ppermute(edges, "lat", mirror)
    inner, edges = lax.optimization_barrier((inner, edges))
    inside = (MID, COLS)
    *middle, own_edges, own_sigma, own_source = build(
        piece_kernel, "pieces", [inside, inside, (2, LINES, SEND), inside, inside],
        planes + [(2, LINES, SEND)],
        outer_far, inner_far, outer, inner, from_right, from_left, ion_density,
    )
    far_middle = [lax.ppermute(part, "lat", mirror) for part in middle]
    to_chip, to_next = bands_to_send(band, own_edges, far_edges)
    from_chip = lax.ppermute(to_chip, "lat", chip)
    from_next = lax.ppermute(to_next, "lat", beyond)

    theta, first_list, second_list = chebyshev_factors()
    factors = jnp.array([first_list, second_list], jnp.float32)
    potential, drift_east, drift_north, peaks = solve(
        lats * lons, factors, band, own_edges, far_edges, from_chip, from_next,
        own_sigma, own_source, *far_middle,
    )
    peaks = lax.all_to_all(peaks, ("lat", "lon"), 0, 0, tiled=True)
    ion_update = advect(
        band, peaks, drift_east, drift_north, ion_density, from_chip, from_next, from_right, from_left
    )
    return (potential, ion_update)


def solution(mesh):
    spec = P(None, "lat", "lon")
    return jax.shard_map(
        shards,
        mesh=mesh,
        in_specs=(spec,) * 5,
        out_specs=(P("lat", "lon"), spec),
        check_vma=False,
    )
```

```python
import functools

import jax
import jax.numpy as jnp
from jax import lax
from jax.experimental import pallas as pl
from jax.experimental.pallas import tpu as pltpu
from jax.sharding import PartitionSpec as P

LEV = 16
SWEEPS = 16
DAMPING = 0.0001
LOW_BOUND = 0.05
HIGH_BOUND = 2.0
COURANT = 0.8
MOBILITY = (1.0, 0.6, 0.3)

LANES = 128
ROWS = 128
COLS = 512
TILES = COLS // LANES
WIDE = COLS + LANES
SEND = WIDE + LANES
PART = COLS // 2
EDGE = 16
HALO = 24
MID = ROWS - 2 * EDGE
EXT = ROWS + 2 * HALO
SIGMA_PLUS = 2 * EDGE
CURRENT = SIGMA_PLUS + 1
IONS = SIGMA_PLUS + 2
NORTH = SIGMA_PLUS + 5
LINES = SIGMA_PLUS + 8
CHUNK = 32
VMEM_BYTES = 32 * 1024 * 1024
COLUMN_BYTES = 51 * 1024 * 1024


def chebyshev_factors():
    theta = 0.5 * (HIGH_BOUND + LOW_BOUND)
    delta = 0.5 * (HIGH_BOUND - LOW_BOUND)
    sigma_one = theta / delta
    rho_prev = 1.0 / sigma_one
    first_list = []
    second_list = []
    for sweep in range(SWEEPS):
        rho_next = 1.0 / (2.0 * sigma_one - rho_prev)
        first_list.append(rho_next * rho_prev)
        second_list.append(2.0 * rho_next / delta)
        rho_prev = rho_next
    return (theta, first_list, second_list)


def lane_index(rows):
    return lax.broadcasted_iota(jnp.int32, (rows, LANES), 1)


def row_index(rows, cols=LANES):
    return lax.broadcasted_iota(jnp.int32, (rows, cols), 0)


def reversed_rows(tile):
    row = row_index(8, tile.shape[1])
    tile = pltpu.roll(tile, 4, 0)
    tile = jnp.where((row & 2) == 0, pltpu.roll(tile, 6, 0), pltpu.roll(tile, 2, 0))
    return jnp.where((row & 1) == 0, pltpu.roll(tile, 7, 0), pltpu.roll(tile, 1, 0))


def shifted(tiles, to_right):
    count = len(tiles)
    lane = lane_index(tiles[0].shape[0])
    if to_right:
        turned = [pltpu.roll(tile, 1, 1) for tile in tiles]
        return [jnp.where(lane == 0, turned[t - 1], turned[t]) for t in range(count)]
    turned = [pltpu.roll(tile, LANES - 1, 1) for tile in tiles]
    return [jnp.where(lane == LANES - 1, turned[(t + 1) % count], turned[t]) for t in range(count)]


def local_source(east, north, source, start, wanted):
    rows = slice(start, start + 8)
    lane = lane_index(8)
    row = row_index(8)
    zero = jnp.zeros((8, LANES), jnp.float32)
    tiles = east.shape[1] // LANES
    for t in wanted:
        span = slice(t * LANES, (t + 1) * LANES)
        tile = east[rows, span]
        left = right = zero
        if t:
            left = pltpu.roll(east[rows, (t - 1) * LANES : t * LANES], 1, 1)
        if t < tiles - 1:
            right = pltpu.roll(east[rows, (t + 1) * LANES : (t + 2) * LANES], LANES - 1, 1)
        before = jnp.where(lane == 0, left, pltpu.roll(tile, 1, 1))
        after = jnp.where(lane == LANES - 1, right, pltpu.roll(tile, LANES - 1, 1))
        here = north[rows, span]
        above = north[start - 8 : start, span][7:8] if start else zero[:1]
        below = north[start + 8 : start + 16, span][:1] if start + 8 < ROWS else zero[:1]
        up = jnp.where(row == 0, above, pltpu.roll(here, 1, 0))
        down = jnp.where(row == 7, below, pltpu.roll(here, 7, 0))
        source[rows, span] = 0.5 * (after - before) + 0.5 * (down - up)


def put_lanes(tile, source, at, first, count):
    lane = lane_index(tile.shape[0])
    turn = (first - at) % LANES
    moved = pltpu.roll(source, turn, 1) if turn else source
    return jnp.where((lane >= first) & (lane < first + count), moved, tile)


def write_strips(sums, source, strips):
    sigma, east, north = (sums.at[0], sums.at[1], sums.at[2])
    for start in range(0, ROWS, 8):
        local_source(east, north, source, start, (0, 1))
    row = row_index(8)
    for side, out in enumerate(strips):
        span = slice(side * LANES, (side + 1) * LANES)
        near = side * (LANES - EDGE)
        strip = jnp.zeros((ROWS, LANES), jnp.float32)
        strip = put_lanes(strip, sigma[:, span], near, 0, EDGE)
        strip = put_lanes(strip, source[:, span], near, EDGE, EDGE)
        strip = put_lanes(strip, sigma[:, span], LANES - EDGE - 1 if side else EDGE, SIGMA_PLUS, 1)
        strip = put_lanes(strip, east[:, span], side * (LANES - 1), CURRENT, 1)
        turned = strip.T
        out[:SIGMA_PLUS] = turned[:SIGMA_PLUS]
        tile = turned[SIGMA_PLUS:LINES]
        tile = jnp.where(row == NORTH - SIGMA_PLUS, north[0:8, span][:1], tile)
        out[SIGMA_PLUS:] = jnp.where(row == NORTH + 1 - SIGMA_PLUS, north[ROWS - 8 :, span][7:8], tile)


def sum_levels(fields, spans, held, arrived, own, far):
    steps = ROWS // CHUNK

    def copies(step):
        rows = pl.ds(pl.multiple_of(step * CHUNK, CHUNK), CHUNK)
        out = []
        for i, field in enumerate(fields):
            at = 0
            for j, (first, width) in enumerate(spans):
                source = field.at[:, rows, pl.ds(first, width)]
                target = held.at[i, :, rows, pl.ds(at, width)]
                out.append(pltpu.make_async_copy(source, target, arrived.at[i, step, j]))
                at += width
        return out

    for step in range(steps):
        for copy in copies(step):
            copy.start()

    def body(step, _):
        for copy in copies(step):
            copy.wait()
        for half in range(CHUNK // 8):
            near = pl.ds(pl.multiple_of(step * CHUNK + half * 8, 8), 8)
            away = pl.ds(pl.multiple_of(ROWS - 8 - step * CHUNK - half * 8, 8), 8)
            totals = [jnp.zeros((8, PART), jnp.float32) for _ in range(3)]
            for level in range(LEV):
                layer = (0.5 + level / LEV) / LEV
                along = layer * held[0, level, near, :]
                across = layer * held[1, level, near, :]
                wind_e = held[2, level, near, :]
                wind_n = held[3, level, near, :]
                totals[0] = totals[0] + along
                totals[1] = totals[1] + (along * wind_e + across * wind_n)
                totals[2] = totals[2] + (along * wind_n - across * wind_e)
            for i, total in enumerate(totals):
                own[i, near, :] = total
                far[i, away, :] = reversed_rows(total)
        return 0

    lax.fori_loop(0, steps, body, 0)


def outer_kernel(
    pedersen, hall, east_wind, north_wind, to_left, to_right, own, far, held, arrived, source
):
    spans = ((0, LANES), (COLS - LANES, LANES))
    sum_levels((pedersen, hall, east_wind, north_wind), spans, held, arrived, own, far)
    for v, sums in enumerate((own, far)):
        rows = pl.ds(v * LINES, LINES)
        write_strips(sums, source, (to_left.at[rows], to_right.at[rows]))


def ion_kernel(left, right, ions, to_left, to_right):
    row = row_index(8)
    for side, strip, out in ((0, left, to_left), (1, right, to_right)):
        at = side * (COLS - LANES)
        tile = strip[SIGMA_PLUS:LINES]
        for s in range(3):
            turned = ions[s, :, at : at + LANES].T
            line = turned[LANES - 1 :] if side else turned[:1]
            tile = jnp.where(row == IONS - SIGMA_PLUS + s, line, tile)
        out[...] = strip[...]
        out[SIGMA_PLUS:LINES] = tile


def inner_kernel(pedersen, hall, east_wind, north_wind, own, far, held, arrived):
    spans = ((LANES, PART),)
    sum_levels((pedersen, hall, east_wind, north_wind), spans, held, arrived, own, far)


def level_sums(kernel, name, shapes, scratch, parts, *fields):
    sums = jax.ShapeDtypeStruct((3, ROWS, PART), jnp.float32)
    out = [jax.ShapeDtypeStruct(shape, jnp.float32) for shape in shapes] + [sums, sums]
    steps = ROWS // CHUNK
    return pl.pallas_call(
        kernel,
        in_specs=[pl.BlockSpec(memory_space=pltpu.HBM)] * len(fields),
        out_specs=[pl.BlockSpec(memory_space=pltpu.VMEM)] * len(out),
        out_shape=out,
        scratch_shapes=[pltpu.VMEM((4, LEV, ROWS, PART), jnp.float32)]
        + [pltpu.SemaphoreType.DMA((4, steps, parts))]
        + [pltpu.VMEM(shape, jnp.float32) for shape in scratch],
        compiler_params=pltpu.CompilerParams(vmem_limit_bytes=COLUMN_BYTES),
        cost_estimate=pl.CostEstimate(flops=1 << 23, bytes_accessed=1 << 23, transcendentals=0),
        name=name,
    )(*fields)


def turned_back(strip):
    rest = jnp.zeros((LANES - LINES, LANES), jnp.float32)
    return jnp.concatenate([strip[...], rest], 0).T


def gather_columns(outer, inner, fields):
    for i, field in enumerate(fields):
        field[:, :LANES] = outer[i, :, :LANES]
        field[:, LANES : COLS - LANES] = inner[i]
        field[:, COLS - LANES :] = outer[i, :, LANES:]


def write_edges(fields, from_right, from_left, ions, source, edges, everything):
    sigma, east, north = fields
    last = COLS - LANES
    for start in range(0, ROWS, 8):
        outer = everything or start < EDGE or start >= ROWS - EDGE
        local_source(east, north, source, start, range(TILES) if outer else (0, TILES - 1))
    right, left = (turned_back(from_right), turned_back(from_left))
    blank = jnp.zeros((ROWS, LANES), jnp.float32)
    sigma_x = put_lanes(blank, right, 0, 0, EDGE)
    sigma_x = put_lanes(sigma_x, right, SIGMA_PLUS, EDGE, 1)
    sigma_x = put_lanes(sigma_x, left, 0, LANES - EDGE, EDGE)
    sigma_x = put_lanes(sigma_x, left, SIGMA_PLUS, LANES - EDGE - 1, 1)
    source_x = put_lanes(blank, right, EDGE, 0, EDGE)
    source_x = put_lanes(source_x, left, EDGE, LANES - EDGE, EDGE)
    source_x = source_x - 0.5 * put_lanes(blank, east[:, last:], LANES - 1, 0, 1)
    source_x = source_x + 0.5 * put_lanes(blank, east[:, :LANES], 0, LANES - 1, 1)
    source[:, :LANES] += put_lanes(blank, -0.5 * left, CURRENT, 0, 1)
    source[:, last:] += put_lanes(blank, 0.5 * right, CURRENT, LANES - 1, 1)

    lane = lane_index(1)
    row = row_index(8)
    wide = row_index(8, COLS)
    for side in range(2):
        first = side * (ROWS - EDGE)
        rows = slice(first, first + EDGE)
        edges[side, :EDGE, :COLS] = sigma[rows]
        edges[side, EDGE:SIGMA_PLUS, :COLS] = source[rows]
        edges[side, :EDGE, COLS:WIDE] = sigma_x[rows]
        edges[side, EDGE:SIGMA_PLUS, COLS:WIDE] = source_x[rows]
        if side == 0:
            further, line = (sigma[EDGE : EDGE + 8][:1], north[0:8][:1])
            further_x = sigma_x[EDGE : EDGE + 1]
        else:
            further, line = (sigma[first - 8 : first][7:8], north[ROWS - 8 :][7:8])
            further_x = sigma_x[first - 1 : first]
        tile = jnp.where(wide == 0, further, 0.0)
        tile = jnp.where(wide == CURRENT - SIGMA_PLUS, line, tile)
        if ions is not None:
            for s in range(3):
                line = ions[s, ROWS - 8 :][7:8] if side else ions[s, :8][:1]
                tile = jnp.where(wide == IONS - SIGMA_PLUS + s, line, tile)
        edges[side, SIGMA_PLUS:, :COLS] = tile
        line = NORTH - SIGMA_PLUS + side
        north_x = jnp.where(
            lane < LANES // 2, from_right[SIGMA_PLUS:][line:][:1], from_left[SIGMA_PLUS:][line:][:1]
        )
        tile = jnp.where(row == 0, further_x, 0.0)
        edges[side, SIGMA_PLUS:, COLS:WIDE] = jnp.where(row == CURRENT - SIGMA_PLUS, north_x, tile)
        strip = put_lanes(blank, sigma_x, side * (LANES - EDGE - 1), 0, EDGE + 1)
        strip = put_lanes(strip, source_x, side * (LANES - EDGE), EDGE + 1, EDGE)
        edges[side, :, WIDE:] = strip.T[:LINES]


def far_kernel(outer, inner, from_right, from_left, edges, sigma, east, north, source):
    fields = (sigma, east, north)
    gather_columns(outer, inner, fields)
    rows = pl.ds(LINES, LINES)
    write_edges(fields, from_right.at[rows], from_left.at[rows], None, source, edges, False)


def piece_kernel(
    outer_far, inner_far, outer, inner, from_right, from_left, ions,
    far_sigma, far_source, own_edges, own_sigma, own_source, sigma, east, north, source, spare,
):
    fields = (sigma, east, north)
    for v, sums, out in (
        (1, (outer_far, inner_far), (far_sigma, far_source)),
        (0, (outer, inner), (own_sigma, own_source)),
    ):
        gather_columns(*sums, fields)
        rows = pl.ds(v * LINES, LINES)
        write_edges(
            fields, from_right.at[rows], from_left.at[rows], None if v else ions, source,
            spare if v else own_edges, True,
        )
        out[0][...] = sigma[EDGE : ROWS - EDGE]
        out[1][...] = source[EDGE : ROWS - EDGE]


def build(kernel, name, shapes, scratch, *fields):
    whole = pl.BlockSpec(memory_space=pltpu.VMEM)
    return pl.pallas_call(
        kernel,
        in_specs=[whole] * len(fields),
        out_specs=[whole] * len(shapes),
        out_shape=[jax.ShapeDtypeStruct(shape, jnp.float32) for shape in shapes],
        scratch_shapes=[pltpu.VMEM(shape, jnp.float32) for shape in scratch],
        compiler_params=pltpu.CompilerParams(vmem_limit_bytes=VMEM_BYTES),
        name=name,
    )(*fields)


def band_kernel(own, far, to_chip, to_next):
    odd = lax.rem(lax.axis_index("lat"), 2) == 1
    top, bottom = (own[side, :, :WIDE] + far[side, :, :WIDE] for side in range(2))
    to_chip[...] = jnp.where(odd, top, bottom)
    to_next[...] = jnp.where(odd, bottom, top)


def solve_kernel(
    factors, own_edges, far_edges, from_chip, from_next,
    own_sigma, own_source, far_sigma, far_source,
    potential, drift_east, drift_north, fastest,
    sigma, sigma_next, sigma_prev, half_inverse, scaled_source, update, field_a, field_b, carried_a, carried_b,
    ours, theirs,
):
    theta = 0.5 * (HIGH_BOUND + LOW_BOUND)
    fields = (field_a, field_b)
    fluxes = (carried_a, carried_b)
    band = lax.axis_index("lat")
    odd = lax.rem(band, 2) == 1
    ours[...] = own_edges[:, :, :WIDE] + far_edges[:, :, :WIDE]
    theirs[0] = jnp.where(odd, from_chip[...], from_next[...])
    theirs[1] = jnp.where(odd, from_next[...], from_chip[...])
    top, bottom = (ours.at[0], ours.at[1])
    above, below = (theirs.at[0], theirs.at[1])
    count = TILES + 1
    spans = [slice(t * LANES, (t + 1) * LANES) for t in range(count)]
    middle = slice(EDGE, ROWS - EDGE)
    row = row_index(8)
    low = HALO + ROWS

    blank = jnp.zeros((ROWS, LANES), jnp.float32)
    right = turned_back(own_edges[0, :, WIDE:] + far_edges[0, :, WIDE:])
    left = turned_back(own_edges[1, :, WIDE:] + far_edges[1, :, WIDE:])
    sigma_x = put_lanes(blank, right, 0, 0, EDGE + 1)
    sigma_x = put_lanes(sigma_x, left, 0, LANES - EDGE - 1, EDGE + 1)
    source_x = put_lanes(blank, right, EDGE + 1, 0, EDGE)
    source_x = put_lanes(source_x, left, EDGE + 1, LANES - EDGE, EDGE)

    for t in range(count):
        span = spans[t]
        for piece, at in ((above, HALO - EDGE), (top, HALO), (bottom, low - EDGE), (below, low)):
            sigma[t, at : at + EDGE] = piece[:EDGE, span]
            scaled_source[t, at : at + EDGE] = piece[EDGE : 2 * EDGE, span]
        outer = above[SIGMA_PLUS:, span][:1]
        sigma[t, :8] = jnp.where(row == 7, outer, 0.0)
        outer = below[SIGMA_PLUS:, span][:1]
        sigma[t, EXT - 8 :] = jnp.where(row == 0, outer, 0.0)
        inner = slice(HALO + EDGE, low - EDGE)
        if t < TILES:
            sigma[t, inner] = own_sigma[:, span] + far_sigma[:, span]
            source = own_source[:, span] + far_source[:, span]
        else:
            sigma[t, inner] = sigma_x[middle]
            source = source_x[middle]
        scaled_source[t, inner] = source
        for at, spot, piece, half in (
            (HALO - 8, 7, top, 0.5),
            (HALO, 0, above, -0.5),
            (low - 8, 7, below, 0.5),
            (low, 0, bottom, -0.5),
        ):
            line = half * piece[SIGMA_PLUS:, span][CURRENT - SIGMA_PLUS :][:1]
            tile = scaled_source[t, at : at + 8]
            scaled_source[t, at : at + 8] = tile + jnp.where(row == spot, line, 0.0)

    first_band = band == 0
    last_band = band == lax.axis_size("lat") - 1
    blank = jnp.zeros((8, LANES), jnp.float32)
    for t in range(count):
        for slot in range(2):
            for at in (0, EXT - 8):
                fields[slot][t, at : at + 8] = blank
                fluxes[slot][t, at : at + 8] = blank

    for start in range(8, EXT - 8, 8):
        here = [sigma[t, start : start + 8] for t in range(count)]
        sides = [sigma[t, start - 1 : start + 7] + sigma[t, start + 1 : start + 9] for t in range(count)]
        tall = [here[t] + 0.5 * sides[t] for t in range(count)]
        left = shifted(tall, True)
        right = shifted(tall, False)
        following = shifted(here, False)
        preceding = shifted(here, True)
        outside = None
        if start < HALO:
            outside = first_band
        if start >= HALO + ROWS:
            outside = last_band
        for t in range(count):
            diagonal = 0.5 * (6.0 * here[t] + (sides[t] + (left[t] + right[t]))) + DAMPING
            inverse = 1.0 / diagonal
            if outside is not None:
                inverse = jnp.where(outside, 0.0, inverse)
            source = scaled_source[t, start : start + 8] * inverse
            initial = source * (1.0 / theta)
            sigma_next[t, start : start + 8] = following[t]
            sigma_prev[t, start : start + 8] = preceding[t]
            half_inverse[t, start : start + 8] = 0.5 * inverse
            scaled_source[t, start : start + 8] = source
            update[t, start : start + 8] = initial
            field_b[t, start : start + 8] = initial
            carried_b[t, start : start + 8] = here[t] * initial

    def sweep(k, now, later, low, high):
        field_now, carried_now = (fields[now], fluxes[now])
        field_later, carried_later = (fields[later], fluxes[later])
        keep = factors[k - 1]
        gain = factors[SWEEPS + k - 1]
        for start in range(low, high, 8):
            rows = slice(start, start + 8)
            upper = slice(start - 1, start + 7)
            lower = slice(start + 1, start + 9)
            centre, eastward, westward = ([], [], [])
            for t in range(count):
                value = field_now[t, rows]
                flux = carried_now[t, rows]
                value_sides = field_now[t, upper] + field_now[t, lower]
                flux_sides = carried_now[t, upper] + carried_now[t, lower]
                tall = value + 0.5 * value_sides
                flux_tall = flux + 0.5 * flux_sides
                centre.append(sigma[t, rows] * value_sides + flux_sides)
                eastward.append(sigma_next[t, rows] * tall + flux_tall)
                westward.append(sigma_prev[t, rows] * tall + flux_tall)
            from_west = shifted(eastward, True)
            from_east = shifted(westward, False)
            for t in range(count):
                total = centre[t] + (from_west[t] + from_east[t])
                value = field_now[t, rows]
                residual = (scaled_source[t, rows] - value) + half_inverse[t, rows] * total
                step = keep * update[t, rows] + gain * residual
                update[t, rows] = step
                value = value + step
                field_later[t, rows] = value
                carried_later[t, rows] = sigma[t, rows] * value

    def early(pair, _):
        sweep(2 * pair + 1, 1, 0, 8, EXT - 8)
        sweep(2 * pair + 2, 0, 1, 8, EXT - 8)
        return 0

    def late(pair, _):
        sweep(2 * pair + 9, 1, 0, 16, EXT - 16)
        sweep(2 * pair + 10, 0, 1, 16, EXT - 16)
        return 0

    lax.fori_loop(0, 4, early, 0)
    lax.fori_loop(0, 3, late, 0)
    sweep(15, 1, 0, 16, EXT - 16)

    last = fields[SWEEPS % 2]
    top_speed = jnp.zeros((8, LANES), jnp.float32)
    for start in range(HALO, HALO + ROWS, 8):
        rows = slice(start, start + 8)
        out = slice(start - HALO, start - HALO + 8)
        tiles = [last[t, rows] for t in range(count)]
        west = shifted(tiles, True)
        east = shifted(tiles, False)
        for t in range(TILES):
            potential[out, spans[t]] = tiles[t]
            lift = -0.5 * (last[t, start + 1 : start + 9] - last[t, start - 1 : start + 7])
            shove = 0.5 * (east[t] - west[t])
            drift_east[out, spans[t]] = lift
            drift_north[out, spans[t]] = shove
            top_speed = jnp.maximum(top_speed, jnp.abs(lift) + jnp.abs(shove))
    peak = jnp.max(top_speed, axis=1, keepdims=True)
    peak = jnp.max(peak, axis=0, keepdims=True)
    fastest[...] = jnp.broadcast_to(peak[None], fastest.shape)


def solve(peers, *fields):
    shapes = [(ROWS, COLS)] * 3 + [(peers, 1, LANES)]
    plane = (TILES + 1, EXT, LANES)
    memory = pltpu.VMEM(plane, jnp.float32)
    return pl.pallas_call(
        solve_kernel,
        in_specs=[pl.BlockSpec(memory_space=pltpu.VMEM)] * len(fields),
        out_specs=[pl.BlockSpec(memory_space=pltpu.VMEM)] * 4,
        out_shape=[jax.ShapeDtypeStruct(shape, jnp.float32) for shape in shapes],
        scratch_shapes=[memory] * 10 + [pltpu.VMEM((2, LINES, WIDE), jnp.float32)] * 2,
        compiler_params=pltpu.CompilerParams(vmem_limit_bytes=VMEM_BYTES),
        name="potential_solve",
    )(*fields)


def advect_kernel(
    fastest, drift_east, drift_north, ions, from_chip, from_next, from_right, from_left, out
):
    odd = lax.rem(lax.axis_index("lat"), 2) == 1
    above = jnp.where(odd, from_chip[SIGMA_PLUS:, :COLS], from_next[SIGMA_PLUS:, :COLS])
    below = jnp.where(odd, from_next[SIGMA_PLUS:, :COLS], from_chip[SIGMA_PLUS:, :COLS])
    peak = jnp.max(fastest[...], axis=0)
    peak = jnp.max(peak, axis=1, keepdims=True)
    time_step = COURANT / (peak + 1e-06)
    lane = lane_index(ROWS)
    wide = row_index(ROWS, LANES)
    beyond_right, beyond_left = (turned_back(from_right[:LINES]), turned_back(from_left[:LINES]))
    for s in range(3):
        pace = MOBILITY[s] * time_step
        tiles = [ions[s, :, t * LANES : (t + 1) * LANES] for t in range(TILES)]
        left = [pltpu.roll(tile, 1, 1) for tile in tiles]
        right = [pltpu.roll(tile, LANES - 1, 1) for tile in tiles]
        edge_right = pltpu.roll(beyond_right, LANES - 1 - IONS - s, 1)
        edge_left = pltpu.roll(beyond_left, LANES - IONS - s, 1)
        for t in range(TILES):
            span = slice(t * LANES, (t + 1) * LANES)
            density = tiles[t]
            west = jnp.where(lane == 0, left[t - 1] if t else edge_left, left[t])
            east = jnp.where(lane == LANES - 1, right[t + 1] if t < TILES - 1 else edge_right, right[t])
            behind = above[:, span][IONS - SIGMA_PLUS + s :][:1]
            ahead = below[:, span][IONS - SIGMA_PLUS + s :][:1]
            south = jnp.where(wide == 0, behind, pltpu.roll(density, 1, 0))
            north = jnp.where(wide == ROWS - 1, ahead, pltpu.roll(density, ROWS - 1, 0))
            cross_east = pace * drift_east[:, span]
            cross_north = pace * drift_north[:, span]
            result = density - jnp.maximum(cross_east, 0.0) * (density - west)
            result = result - jnp.minimum(cross_east, 0.0) * (east - density)
            result = result - jnp.maximum(cross_north, 0.0) * (density - south)
            result = result - jnp.minimum(cross_north, 0.0) * (north - density)
            out[s, :, span] = result


def shards(pedersen, hall_conductivity, east_wind, north_wind, ion_density):
    lats = lax.axis_size("lat")
    lons = lax.axis_size("lon")
    mirror = [(i, lats - 1 - i) for i in range(lats)]
    eastward = [(i, (i + 1) % lons) for i in range(lons)]
    westward = [(j, i) for i, j in eastward]
    chip = [(i, i ^ 1) for i in range(lats)]
    beyond = [(i, i + 1 if i % 2 else i - 1) for i in range(1, lats - 1)]

    levels = (pedersen, hall_conductivity, east_wind, north_wind)
    strip = (2 * LINES, LANES)
    left, right, outer, outer_far = level_sums(
        outer_kernel, "outer_sums", [strip] * 2, [(ROWS, PART)], 2, *levels
    )
    to_left, to_right = build(ion_kernel, "lon_strips", [strip] * 2, [], left, right, ion_density)
    from_right = lax.ppermute(to_left, "lon", westward)
    from_left = lax.ppermute(to_right, "lon", eastward)
    inner, inner_far = level_sums(inner_kernel, "inner_sums", [], [], 1, *levels)
    planes = [(ROWS, COLS)] * 4
    (edges,) = build(
        far_kernel, "wide_edges", [(2, LINES, SEND)], planes, outer_far, inner_far, from_right, from_left
    )
    far_edges = lax.ppermute(edges, "lat", mirror)
    inner, edges = lax.optimization_barrier((inner, edges))
    inside = (MID, COLS)
    *middle, own_edges, own_sigma, own_source = build(
        piece_kernel, "pieces", [inside, inside, (2, LINES, SEND), inside, inside],
        planes + [(2, LINES, SEND)],
        outer_far, inner_far, outer, inner, from_right, from_left, ion_density,
    )
    far_middle = [lax.ppermute(part, "lat", mirror) for part in middle]
    to_chip, to_next = build(band_kernel, "lat_bands", [(LINES, WIDE)] * 2, [], own_edges, far_edges)
    from_chip = lax.ppermute(to_chip, "lat", chip)
    from_next = lax.ppermute(to_next, "lat", beyond)

    theta, first_list, second_list = chebyshev_factors()
    factors = jnp.array(first_list + second_list, jnp.float32)
    factors = jnp.broadcast_to(factors[:, None, None], (2 * SWEEPS, 8, LANES))
    potential, drift_east, drift_north, peaks = solve(
        lats * lons, factors, own_edges, far_edges, from_chip, from_next,
        own_sigma, own_source, *far_middle,
    )
    peaks = lax.all_to_all(peaks, ("lat", "lon"), 0, 0, tiled=True)
    (ion_update,) = build(
        advect_kernel, "ion_advection", [(3, ROWS, COLS)], [],
        peaks, drift_east, drift_north, ion_density, from_chip, from_next, from_right, from_left,
    )
    return (potential, ion_update)


def solution(mesh):
    spec = P(None, "lat", "lon")
    return jax.shard_map(
        shards,
        mesh=mesh,
        in_specs=(spec,) * 5,
        out_specs=(P("lat", "lon"), spec),
        check_vma=False,
    )
```

```python
import functools

import jax
import jax.numpy as jnp
from jax import lax
from jax.experimental import pallas as pl
from jax.experimental.pallas import tpu as pltpu
from jax.sharding import PartitionSpec as P

LEV = 16
SWEEPS = 16
DAMPING = 0.0001
LOW_BOUND = 0.05
HIGH_BOUND = 2.0
COURANT = 0.8
MOBILITY = (1.0, 0.6, 0.3)

LANES = 128
ROWS = 128
COLS = 512
TILES = COLS // LANES
WIDE = COLS + LANES
SEND = WIDE + LANES
PART = COLS // 2
EDGE = 16
HALO = 24
MID = ROWS - 2 * EDGE
EXT = ROWS + 2 * HALO
SIGMA_PLUS = 2 * EDGE
CURRENT = SIGMA_PLUS + 1
IONS = SIGMA_PLUS + 2
NORTH = SIGMA_PLUS + 5
LINES = SIGMA_PLUS + 8
CHUNK = 32
VMEM_BYTES = 32 * 1024 * 1024
COLUMN_BYTES = 51 * 1024 * 1024


def chebyshev_factors():
    theta = 0.5 * (HIGH_BOUND + LOW_BOUND)
    delta = 0.5 * (HIGH_BOUND - LOW_BOUND)
    sigma_one = theta / delta
    rho_prev = 1.0 / sigma_one
    first_list = []
    second_list = []
    for sweep in range(SWEEPS):
        rho_next = 1.0 / (2.0 * sigma_one - rho_prev)
        first_list.append(rho_next * rho_prev)
        second_list.append(2.0 * rho_next / delta)
        rho_prev = rho_next
    return (theta, first_list, second_list)


def lane_index(rows):
    return lax.broadcasted_iota(jnp.int32, (rows, LANES), 1)


def row_index(rows, cols=LANES):
    return lax.broadcasted_iota(jnp.int32, (rows, cols), 0)


def reversed_rows(tile):
    row = row_index(8, tile.shape[1])
    tile = pltpu.roll(tile, 4, 0)
    tile = jnp.where((row & 2) == 0, pltpu.roll(tile, 6, 0), pltpu.roll(tile, 2, 0))
    return jnp.where((row & 1) == 0, pltpu.roll(tile, 7, 0), pltpu.roll(tile, 1, 0))


def shifted(tiles, to_right):
    count = len(tiles)
    lane = lane_index(tiles[0].shape[0])
    if to_right:
        turned = [pltpu.roll(tile, 1, 1) for tile in tiles]
        return [jnp.where(lane == 0, turned[t - 1], turned[t]) for t in range(count)]
    turned = [pltpu.roll(tile, LANES - 1, 1) for tile in tiles]
    return [jnp.where(lane == LANES - 1, turned[(t + 1) % count], turned[t]) for t in range(count)]


def local_source(east, north, source, start, wanted):
    rows = slice(start, start + 8)
    lane = lane_index(8)
    row = row_index(8)
    zero = jnp.zeros((8, LANES), jnp.float32)
    tiles = east.shape[1] // LANES
    for t in wanted:
        span = slice(t * LANES, (t + 1) * LANES)
        tile = east[rows, span]
        left = right = zero
        if t:
            left = pltpu.roll(east[rows, (t - 1) * LANES : t * LANES], 1, 1)
        if t < tiles - 1:
            right = pltpu.roll(east[rows, (t + 1) * LANES : (t + 2) * LANES], LANES - 1, 1)
        before = jnp.where(lane == 0, left, pltpu.roll(tile, 1, 1))
        after = jnp.where(lane == LANES - 1, right, pltpu.roll(tile, LANES - 1, 1))
        here = north[rows, span]
        above = north[start - 8 : start, span][7:8] if start else zero[:1]
        below = north[start + 8 : start + 16, span][:1] if start + 8 < ROWS else zero[:1]
        up = jnp.where(row == 0, above, pltpu.roll(here, 1, 0))
        down = jnp.where(row == 7, below, pltpu.roll(here, 7, 0))
        source[rows, span] = 0.5 * (after - before) + 0.5 * (down - up)


def put_lanes(tile, source, at, first, count):
    lane = lane_index(tile.shape[0])
    turn = (first - at) % LANES
    moved = pltpu.roll(source, turn, 1) if turn else source
    return jnp.where((lane >= first) & (lane < first + count), moved, tile)


def write_strips(sums, source, strips):
    sigma, east, north = (sums.at[0], sums.at[1], sums.at[2])
    for start in range(0, ROWS, 8):
        local_source(east, north, source, start, (0, 1))
    row = row_index(8)
    for side, out in enumerate(strips):
        span = slice(side * LANES, (side + 1) * LANES)
        near = side * (LANES - EDGE)
        strip = jnp.zeros((ROWS, LANES), jnp.float32)
        strip = put_lanes(strip, sigma[:, span], near, 0, EDGE)
        strip = put_lanes(strip, source[:, span], near, EDGE, EDGE)
        strip = put_lanes(strip, sigma[:, span], LANES - EDGE - 1 if side else EDGE, SIGMA_PLUS, 1)
        strip = put_lanes(strip, east[:, span], side * (LANES - 1), CURRENT, 1)
        turned = strip.T
        out[:SIGMA_PLUS] = turned[:SIGMA_PLUS]
        tile = turned[SIGMA_PLUS:LINES]
        tile = jnp.where(row == NORTH - SIGMA_PLUS, north[0:8, span][:1], tile)
        out[SIGMA_PLUS:] = jnp.where(row == NORTH + 1 - SIGMA_PLUS, north[ROWS - 8 :, span][7:8], tile)


def sum_levels(fields, spans, held, arrived, own, far):
    steps = ROWS // CHUNK

    def copies(step):
        rows = pl.ds(pl.multiple_of(step * CHUNK, CHUNK), CHUNK)
        out = []
        for i, field in enumerate(fields):
            at = 0
            for j, (first, width) in enumerate(spans):
                source = field.at[:, rows, pl.ds(first, width)]
                target = held.at[i, :, rows, pl.ds(at, width)]
                out.append(pltpu.make_async_copy(source, target, arrived.at[i, step, j]))
                at += width
        return out

    for step in range(steps):
        for copy in copies(step):
            copy.start()

    def body(step, _):
        for copy in copies(step):
            copy.wait()
        for half in range(CHUNK // 8):
            near = pl.ds(pl.multiple_of(step * CHUNK + half * 8, 8), 8)
            away = pl.ds(pl.multiple_of(ROWS - 8 - step * CHUNK - half * 8, 8), 8)
            totals = [jnp.zeros((8, PART), jnp.float32) for _ in range(3)]
            for level in range(LEV):
                layer = (0.5 + level / LEV) / LEV
                along = layer * held[0, level, near, :]
                across = layer * held[1, level, near, :]
                wind_e = held[2, level, near, :]
                wind_n = held[3, level, near, :]
                totals[0] = totals[0] + along
                totals[1] = totals[1] + (along * wind_e + across * wind_n)
                totals[2] = totals[2] + (along * wind_n - across * wind_e)
            for i, total in enumerate(totals):
                own[i, near, :] = total
                far[i, away, :] = reversed_rows(total)
        return 0

    lax.fori_loop(0, steps, body, 0)


def outer_kernel(
    pedersen, hall, east_wind, north_wind, to_left, to_right, own, far, held, arrived, source
):
    spans = ((0, LANES), (COLS - LANES, LANES))
    sum_levels((pedersen, hall, east_wind, north_wind), spans, held, arrived, own, far)
    for v, sums in enumerate((own, far)):
        rows = pl.ds(v * LINES, LINES)
        write_strips(sums, source, (to_left.at[rows], to_right.at[rows]))


def ion_kernel(left, right, ions, to_left, to_right):
    row = row_index(8)
    for side, strip, out in ((0, left, to_left), (1, right, to_right)):
        at = side * (COLS - LANES)
        tile = strip[SIGMA_PLUS:LINES]
        for s in range(3):
            turned = ions[s, :, at : at + LANES].T
            line = turned[LANES - 1 :] if side else turned[:1]
            tile = jnp.where(row == IONS - SIGMA_PLUS + s, line, tile)
        out[...] = strip[...]
        out[SIGMA_PLUS:LINES] = tile


def inner_kernel(pedersen, hall, east_wind, north_wind, own, far, held, arrived):
    spans = ((LANES, PART),)
    sum_levels((pedersen, hall, east_wind, north_wind), spans, held, arrived, own, far)


def level_sums(kernel, name, shapes, scratch, parts, *fields):
    sums = jax.ShapeDtypeStruct((3, ROWS, PART), jnp.float32)
    out = [jax.ShapeDtypeStruct(shape, jnp.float32) for shape in shapes] + [sums, sums]
    steps = ROWS // CHUNK
    return pl.pallas_call(
        kernel,
        in_specs=[pl.BlockSpec(memory_space=pltpu.HBM)] * len(fields),
        out_specs=[pl.BlockSpec(memory_space=pltpu.VMEM)] * len(out),
        out_shape=out,
        scratch_shapes=[pltpu.VMEM((4, LEV, ROWS, PART), jnp.float32)]
        + [pltpu.SemaphoreType.DMA((4, steps, parts))]
        + [pltpu.VMEM(shape, jnp.float32) for shape in scratch],
        compiler_params=pltpu.CompilerParams(vmem_limit_bytes=COLUMN_BYTES),
        cost_estimate=pl.CostEstimate(flops=1 << 23, bytes_accessed=1 << 23, transcendentals=0),
        name=name,
    )(*fields)


def turned_back(strip):
    rest = jnp.zeros((LANES - LINES, LANES), jnp.float32)
    return jnp.concatenate([strip[...], rest], 0).T


def gather_columns(outer, inner, fields):
    for i, field in enumerate(fields):
        field[:, :LANES] = outer[i, :, :LANES]
        field[:, LANES : COLS - LANES] = inner[i]
        field[:, COLS - LANES :] = outer[i, :, LANES:]


def write_edges(fields, from_right, from_left, ions, source, edges, everything):
    sigma, east, north = fields
    last = COLS - LANES
    for start in range(0, ROWS, 8):
        outer = everything or start < EDGE or start >= ROWS - EDGE
        local_source(east, north, source, start, range(TILES) if outer else (0, TILES - 1))
    right, left = (turned_back(from_right), turned_back(from_left))
    blank = jnp.zeros((ROWS, LANES), jnp.float32)
    sigma_x = put_lanes(blank, right, 0, 0, EDGE)
    sigma_x = put_lanes(sigma_x, right, SIGMA_PLUS, EDGE, 1)
    sigma_x = put_lanes(sigma_x, left, 0, LANES - EDGE, EDGE)
    sigma_x = put_lanes(sigma_x, left, SIGMA_PLUS, LANES - EDGE - 1, 1)
    source_x = put_lanes(blank, right, EDGE, 0, EDGE)
    source_x = put_lanes(source_x, left, EDGE, LANES - EDGE, EDGE)
    source_x = source_x - 0.5 * put_lanes(blank, east[:, last:], LANES - 1, 0, 1)
    source_x = source_x + 0.5 * put_lanes(blank, east[:, :LANES], 0, LANES - 1, 1)
    source[:, :LANES] += put_lanes(blank, -0.5 * left, CURRENT, 0, 1)
    source[:, last:] += put_lanes(blank, 0.5 * right, CURRENT, LANES - 1, 1)

    lane = lane_index(1)
    row = row_index(8)
    wide = row_index(8, COLS)
    for side in range(2):
        first = side * (ROWS - EDGE)
        rows = slice(first, first + EDGE)
        edges[side, :EDGE, :COLS] = sigma[rows]
        edges[side, EDGE:SIGMA_PLUS, :COLS] = source[rows]
        edges[side, :EDGE, COLS:WIDE] = sigma_x[rows]
        edges[side, EDGE:SIGMA_PLUS, COLS:WIDE] = source_x[rows]
        if side == 0:
            further, line = (sigma[EDGE : EDGE + 8][:1], north[0:8][:1])
            further_x = sigma_x[EDGE : EDGE + 1]
        else:
            further, line = (sigma[first - 8 : first][7:8], north[ROWS - 8 :][7:8])
            further_x = sigma_x[first - 1 : first]
        tile = jnp.where(wide == 0, further, 0.0)
        tile = jnp.where(wide == CURRENT - SIGMA_PLUS, line, tile)
        if ions is not None:
            for s in range(3):
                line = ions[s, ROWS - 8 :][7:8] if side else ions[s, :8][:1]
                tile = jnp.where(wide == IONS - SIGMA_PLUS + s, line, tile)
        edges[side, SIGMA_PLUS:, :COLS] = tile
        line = NORTH - SIGMA_PLUS + side
        north_x = jnp.where(
            lane < LANES // 2, from_right[SIGMA_PLUS:][line:][:1], from_left[SIGMA_PLUS:][line:][:1]
        )
        tile = jnp.where(row == 0, further_x, 0.0)
        edges[side, SIGMA_PLUS:, COLS:WIDE] = jnp.where(row == CURRENT - SIGMA_PLUS, north_x, tile)
        strip = put_lanes(blank, sigma_x, side * (LANES - EDGE - 1), 0, EDGE + 1)
        strip = put_lanes(strip, source_x, side * (LANES - EDGE), EDGE + 1, EDGE)
        edges[side, :, WIDE:] = strip.T[:LINES]


def far_kernel(outer, inner, from_right, from_left, edges, sigma, east, north, source):
    fields = (sigma, east, north)
    gather_columns(outer, inner, fields)
    rows = pl.ds(LINES, LINES)
    write_edges(fields, from_right.at[rows], from_left.at[rows], None, source, edges, False)


def piece_kernel(
    outer_far, inner_far, outer, inner, from_right, from_left, ions,
    far_sigma, far_source, own_edges, own_sigma, own_source, sigma, east, north, source, spare,
):
    fields = (sigma, east, north)
    for v, sums, out in (
        (1, (outer_far, inner_far), (far_sigma, far_source)),
        (0, (outer, inner), (own_sigma, own_source)),
    ):
        gather_columns(*sums, fields)
        rows = pl.ds(v * LINES, LINES)
        write_edges(
            fields, from_right.at[rows], from_left.at[rows], None if v else ions, source,
            spare if v else own_edges, True,
        )
        out[0][...] = sigma[EDGE : ROWS - EDGE]
        out[1][...] = source[EDGE : ROWS - EDGE]


def build(kernel, name, shapes, scratch, *fields):
    whole = pl.BlockSpec(memory_space=pltpu.VMEM)
    return pl.pallas_call(
        kernel,
        in_specs=[whole] * len(fields),
        out_specs=[whole] * len(shapes),
        out_shape=[jax.ShapeDtypeStruct(shape, jnp.float32) for shape in shapes],
        scratch_shapes=[pltpu.VMEM(shape, jnp.float32) for shape in scratch],
        compiler_params=pltpu.CompilerParams(vmem_limit_bytes=VMEM_BYTES),
        name=name,
    )(*fields)


def band_kernel(own, far, to_chip, to_next):
    odd = lax.rem(lax.axis_index("lat"), 2) == 1
    top, bottom = (own[side, :, :WIDE] + far[side, :, :WIDE] for side in range(2))
    to_chip[...] = jnp.where(odd, top, bottom)
    to_next[...] = jnp.where(odd, bottom, top)


def solve_kernel(
    factors, own_edges, far_edges, from_chip, from_next,
    own_sigma, own_source, far_sigma, far_source,
    potential, drift_east, drift_north, fastest,
    sigma, sigma_next, sigma_prev, half_inverse, scaled_source, update, field_a, field_b, carried_a, carried_b,
    ours, theirs,
):
    theta = 0.5 * (HIGH_BOUND + LOW_BOUND)
    fields = (field_a, field_b)
    fluxes = (carried_a, carried_b)
    band = lax.axis_index("lat")
    odd = lax.rem(band, 2) == 1
    ours[...] = own_edges[:, :, :WIDE] + far_edges[:, :, :WIDE]
    theirs[0] = jnp.where(odd, from_chip[...], from_next[...])
    theirs[1] = jnp.where(odd, from_next[...], from_chip[...])
    top, bottom = (ours.at[0], ours.at[1])
    above, below = (theirs.at[0], theirs.at[1])
    count = TILES + 1
    spans = [slice(t * LANES, (t + 1) * LANES) for t in range(count)]
    middle = slice(EDGE, ROWS - EDGE)
    row = row_index(8)
    low = HALO + ROWS

    blank = jnp.zeros((ROWS, LANES), jnp.float32)
    right = turned_back(own_edges[0, :, WIDE:] + far_edges[0, :, WIDE:])
    left = turned_back(own_edges[1, :, WIDE:] + far_edges[1, :, WIDE:])
    sigma_x = put_lanes(blank, right, 0, 0, EDGE + 1)
    sigma_x = put_lanes(sigma_x, left, 0, LANES - EDGE - 1, EDGE + 1)
    source_x = put_lanes(blank, right, EDGE + 1, 0, EDGE)
    source_x = put_lanes(source_x, left, EDGE + 1, LANES - EDGE, EDGE)

    for t in range(count):
        span = spans[t]
        for piece, at in ((above, HALO - EDGE), (top, HALO), (bottom, low - EDGE), (below, low)):
            sigma[t, at : at + EDGE] = piece[:EDGE, span]
            scaled_source[t, at : at + EDGE] = piece[EDGE : 2 * EDGE, span]
        outer = above[SIGMA_PLUS:, span][:1]
        sigma[t, :8] = jnp.where(row == 7, outer, 0.0)
        outer = below[SIGMA_PLUS:, span][:1]
        sigma[t, EXT - 8 :] = jnp.where(row == 0, outer, 0.0)
        inner = slice(HALO + EDGE, low - EDGE)
        if t < TILES:
            sigma[t, inner] = own_sigma[:, span] + far_sigma[:, span]
            source = own_source[:, span] + far_source[:, span]
        else:
            sigma[t, inner] = sigma_x[middle]
            source = source_x[middle]
        scaled_source[t, inner] = source
        for at, spot, piece, half in (
            (HALO - 8, 7, top, 0.5),
            (HALO, 0, above, -0.5),
            (low - 8, 7, below, 0.5),
            (low, 0, bottom, -0.5),
        ):
            line = half * piece[SIGMA_PLUS:, span][CURRENT - SIGMA_PLUS :][:1]
            tile = scaled_source[t, at : at + 8]
            scaled_source[t, at : at + 8] = tile + jnp.where(row == spot, line, 0.0)

    first_band = band == 0
    last_band = band == lax.axis_size("lat") - 1
    blank = jnp.zeros((8, LANES), jnp.float32)
    for t in range(count):
        for slot in range(2):
            for at in (0, EXT - 8):
                fields[slot][t, at : at + 8] = blank
                fluxes[slot][t, at : at + 8] = blank

    for start in range(8, EXT - 8, 8):
        here = [sigma[t, start : start + 8] for t in range(count)]
        sides = [sigma[t, start - 1 : start + 7] + sigma[t, start + 1 : start + 9] for t in range(count)]
        tall = [here[t] + 0.5 * sides[t] for t in range(count)]
        left = shifted(tall, True)
        right = shifted(tall, False)
        following = shifted(here, False)
        preceding = shifted(here, True)
        outside = None
        if start < HALO:
            outside = first_band
        if start >= HALO + ROWS:
            outside = last_band
        for t in range(count):
            diagonal = 0.5 * (6.0 * here[t] + (sides[t] + (left[t] + right[t]))) + DAMPING
            inverse = 1.0 / diagonal
            if outside is not None:
                inverse = jnp.where(outside, 0.0, inverse)
            source = scaled_source[t, start : start + 8] * inverse
            initial = source * (1.0 / theta)
            sigma_next[t, start : start + 8] = following[t]
            sigma_prev[t, start : start + 8] = preceding[t]
            half_inverse[t, start : start + 8] = 0.5 * inverse
            scaled_source[t, start : start + 8] = source
            update[t, start : start + 8] = initial
            field_b[t, start : start + 8] = initial
            carried_b[t, start : start + 8] = here[t] * initial

    def sweep(k, now, later, low, high):
        field_now, carried_now = (fields[now], fluxes[now])
        field_later, carried_later = (fields[later], fluxes[later])
        keep = factors[k - 1]
        gain = factors[SWEEPS + k - 1]
        for start in range(low, high, 8):
            rows = slice(start, start + 8)
            upper = slice(start - 1, start + 7)
            lower = slice(start + 1, start + 9)
            centre, eastward, westward = ([], [], [])
            for t in range(count):
                value = field_now[t, rows]
                flux = carried_now[t, rows]
                value_sides = field_now[t, upper] + field_now[t, lower]
                flux_sides = carried_now[t, upper] + carried_now[t, lower]
                tall = value + 0.5 * value_sides
                flux_tall = flux + 0.5 * flux_sides
                centre.append(sigma[t, rows] * value_sides + flux_sides)
                eastward.append(sigma_next[t, rows] * tall + flux_tall)
                westward.append(sigma_prev[t, rows] * tall + flux_tall)
            from_west = shifted(eastward, True)
            from_east = shifted(westward, False)
            for t in range(count):
                total = centre[t] + (from_west[t] + from_east[t])
                value = field_now[t, rows]
                residual = (scaled_source[t, rows] - value) + half_inverse[t, rows] * total
                step = keep * update[t, rows] + gain * residual
                update[t, rows] = step
                value = value + step
                field_later[t, rows] = value
                carried_later[t, rows] = sigma[t, rows] * value

    def early(pair, _):
        sweep(2 * pair + 1, 1, 0, 8, EXT - 8)
        sweep(2 * pair + 2, 0, 1, 8, EXT - 8)
        return 0

    def late(pair, _):
        sweep(2 * pair + 9, 1, 0, 16, EXT - 16)
        sweep(2 * pair + 10, 0, 1, 16, EXT - 16)
        return 0

    lax.fori_loop(0, 4, early, 0)
    lax.fori_loop(0, 3, late, 0)
    sweep(15, 1, 0, 16, EXT - 16)

    last = fields[SWEEPS % 2]
    top_speed = jnp.zeros((8, LANES), jnp.float32)
    for start in range(HALO, HALO + ROWS, 8):
        rows = slice(start, start + 8)
        out = slice(start - HALO, start - HALO + 8)
        tiles = [last[t, rows] for t in range(count)]
        west = shifted(tiles, True)
        east = shifted(tiles, False)
        for t in range(TILES):
            potential[out, spans[t]] = tiles[t]
            lift = -0.5 * (last[t, start + 1 : start + 9] - last[t, start - 1 : start + 7])
            shove = 0.5 * (east[t] - west[t])
            drift_east[out, spans[t]] = lift
            drift_north[out, spans[t]] = shove
            top_speed = jnp.maximum(top_speed, jnp.abs(lift) + jnp.abs(shove))
    peak = jnp.max(top_speed, axis=1, keepdims=True)
    peak = jnp.max(peak, axis=0, keepdims=True)
    fastest[...] = jnp.broadcast_to(peak[None], fastest.shape)


def solve(peers, *fields):
    shapes = [(ROWS, COLS)] * 3 + [(peers, 1, LANES)]
    plane = (TILES + 1, EXT, LANES)
    memory = pltpu.VMEM(plane, jnp.float32)
    return pl.pallas_call(
        solve_kernel,
        in_specs=[pl.BlockSpec(memory_space=pltpu.VMEM)] * len(fields),
        out_specs=[pl.BlockSpec(memory_space=pltpu.VMEM)] * 4,
        out_shape=[jax.ShapeDtypeStruct(shape, jnp.float32) for shape in shapes],
        scratch_shapes=[memory] * 10 + [pltpu.VMEM((2, LINES, WIDE), jnp.float32)] * 2,
        compiler_params=pltpu.CompilerParams(vmem_limit_bytes=VMEM_BYTES),
        name="potential_solve",
    )(*fields)


def advect_kernel(
    fastest, drift_east, drift_north, ions, from_chip, from_next, from_right, from_left, out, made, sent
):
    odd = lax.rem(lax.axis_index("lat"), 2) == 1
    above = jnp.where(odd, from_chip[SIGMA_PLUS:, :COLS], from_next[SIGMA_PLUS:, :COLS])
    below = jnp.where(odd, from_next[SIGMA_PLUS:, :COLS], from_chip[SIGMA_PLUS:, :COLS])
    peak = jnp.max(fastest[...], axis=0)
    peak = jnp.max(peak, axis=1, keepdims=True)
    time_step = COURANT / (peak + 1e-06)
    lane = lane_index(8)
    row = row_index(8)
    beyond_right, beyond_left = (turned_back(from_right[:LINES]), turned_back(from_left[:LINES]))
    copies = []
    for s in range(3):
        pace = jnp.broadcast_to(MOBILITY[s] * time_step, (8, LANES))
        edge_right = pltpu.roll(beyond_right, LANES - 1 - IONS - s, 1)
        edge_left = pltpu.roll(beyond_left, LANES - IONS - s, 1)
        line = slice(IONS - SIGMA_PLUS + s, IONS - SIGMA_PLUS + s + 1)
        for start in range(0, ROWS, 8):
            rows = slice(start, start + 8)
            tiles = [ions[s, rows, t * LANES : (t + 1) * LANES] for t in range(TILES)]
            left = [edge_left[rows]] + [pltpu.roll(tile, 1, 1) for tile in tiles]
            right = [pltpu.roll(tile, LANES - 1, 1) for tile in tiles] + [edge_right[rows]]
            for t in range(TILES):
                span = slice(t * LANES, (t + 1) * LANES)
                density = tiles[t]
                west = jnp.where(lane == 0, left[t], left[t + 1])
                east = jnp.where(lane == LANES - 1, right[t + 1], right[t])
                behind = ions[s, start - 8 : start, span][7:8] if start else above[line, span]
                ahead = below[line, span]
                if start + 8 < ROWS:
                    ahead = ions[s, start + 8 : start + 16, span][:1]
                south = jnp.where(row == 0, behind, pltpu.roll(density, 1, 0))
                north = jnp.where(row == 7, ahead, pltpu.roll(density, 7, 0))
                cross_east = pace * drift_east[rows, span]
                cross_north = pace * drift_north[rows, span]
                result = density - jnp.maximum(cross_east, 0.0) * (density - west)
                result = result - jnp.minimum(cross_east, 0.0) * (east - density)
                result = result - jnp.maximum(cross_north, 0.0) * (density - south)
                result = result - jnp.minimum(cross_north, 0.0) * (north - density)
                made[s, rows, span] = result
        copies.append(pltpu.make_async_copy(made.at[s], out.at[s], sent.at[s]))
        copies[s].start()
    for copy in copies:
        copy.wait()


def advect(*fields):
    return pl.pallas_call(
        advect_kernel,
        in_specs=[pl.BlockSpec(memory_space=pltpu.VMEM)] * len(fields),
        out_specs=pl.BlockSpec(memory_space=pltpu.HBM),
        out_shape=jax.ShapeDtypeStruct((3, ROWS, COLS), jnp.float32),
        scratch_shapes=[pltpu.VMEM((3, ROWS, COLS), jnp.float32), pltpu.SemaphoreType.DMA((3,))],
        compiler_params=pltpu.CompilerParams(vmem_limit_bytes=VMEM_BYTES),
        name="ion_advection",
    )(*fields)


def shards(pedersen, hall_conductivity, east_wind, north_wind, ion_density):
    lats = lax.axis_size("lat")
    lons = lax.axis_size("lon")
    mirror = [(i, lats - 1 - i) for i in range(lats)]
    eastward = [(i, (i + 1) % lons) for i in range(lons)]
    westward = [(j, i) for i, j in eastward]
    chip = [(i, i ^ 1) for i in range(lats)]
    beyond = [(i, i + 1 if i % 2 else i - 1) for i in range(1, lats - 1)]

    levels = (pedersen, hall_conductivity, east_wind, north_wind)
    strip = (2 * LINES, LANES)
    left, right, outer, outer_far = level_sums(
        outer_kernel, "outer_sums", [strip] * 2, [(ROWS, PART)], 2, *levels
    )
    to_left, to_right = build(ion_kernel, "lon_strips", [strip] * 2, [], left, right, ion_density)
    from_right = lax.ppermute(to_left, "lon", westward)
    from_left = lax.ppermute(to_right, "lon", eastward)
    inner, inner_far = level_sums(inner_kernel, "inner_sums", [], [], 1, *levels)
    planes = [(ROWS, COLS)] * 4
    (edges,) = build(
        far_kernel, "wide_edges", [(2, LINES, SEND)], planes, outer_far, inner_far, from_right, from_left
    )
    far_edges = lax.ppermute(edges, "lat", mirror)
    inner, edges = lax.optimization_barrier((inner, edges))
    inside = (MID, COLS)
    *middle, own_edges, own_sigma, own_source = build(
        piece_kernel, "pieces", [inside, inside, (2, LINES, SEND), inside, inside],
        planes + [(2, LINES, SEND)],
        outer_far, inner_far, outer, inner, from_right, from_left, ion_density,
    )
    far_middle = [lax.ppermute(part, "lat", mirror) for part in middle]
    to_chip, to_next = build(band_kernel, "lat_bands", [(LINES, WIDE)] * 2, [], own_edges, far_edges)
    from_chip = lax.ppermute(to_chip, "lat", chip)
    from_next = lax.ppermute(to_next, "lat", beyond)

    theta, first_list, second_list = chebyshev_factors()
    factors = jnp.array(first_list + second_list, jnp.float32)
    factors = jnp.broadcast_to(factors[:, None, None], (2 * SWEEPS, 8, LANES))
    potential, drift_east, drift_north, peaks = solve(
        lats * lons, factors, own_edges, far_edges, from_chip, from_next,
        own_sigma, own_source, *far_middle,
    )
    peaks = lax.all_to_all(peaks, ("lat", "lon"), 0, 0, tiled=True)
    ion_update = advect(
        peaks, drift_east, drift_north, ion_density, from_chip, from_next, from_right, from_left
    )
    return (potential, ion_update)


def solution(mesh):
    spec = P(None, "lat", "lon")
    return jax.shard_map(
        shards,
        mesh=mesh,
        in_specs=(spec,) * 5,
        out_specs=(P("lat", "lon"), spec),
        check_vma=False,
    )
```
